256 devices in a mesh: gx: 8 (over y, core), gy: 32 (over x, z).
Axes of the slice: x: 4, y: 4, z: 8, core: 2. Of those that a mesh axis runs over, the one named last changes fastest.
Arguments:
- values: bfloat16 [8, 8, 32, 2048], P(None, 'gx', 'gy'), may hold values from -6 to 6
- point_slot: int32 [8, 32, 2048], P('gx', 'gy'), may hold values from 0 to 2047, each once within a row
- leaf_basis: bfloat16 [32, 128, 128, 64], P('gx', 'gy'), may hold values from -0.5 to 0.5
- near_blocks: bfloat16 [32, 128, 9, 128, 128], P('gx', 'gy'), may hold values from -0.1875 to 0.1875
- transfer_leaf: bfloat16 [32, 128, 64, 64], P('gx', 'gy'), may hold values from -0.5 to 0.5
- transfer_mid: bfloat16 [16, 64, 64, 64], P('gx', 'gy'), may hold values from -0.5 to 0.5
- transfer_dev: bfloat16 [8, 32, 64, 64], P('gx', 'gy'), may hold values from -0.5 to 0.5
- transfer_coarse: bfloat16 [4, 16, 64, 64], replicated, may hold values from -0.5 to 0.5
- coupling_leaf: bfloat16 [32, 128, 36, 64, 64], P('gx', 'gy'), may hold values from -0.15625 to 0.15625
- coupling_mid: bfloat16 [16, 64, 36, 64, 64], P('gx', 'gy'), may hold values from -0.15625 to 0.15625
- coupling_dev: bfloat16 [8, 32, 36, 64, 64], P('gx', 'gy'), may hold values from -0.15625 to 0.15625
- coupling_coarse: bfloat16 [8, 32, 36, 16, 64], P('gx', 'gy'), may hold values from -0.15625 to 0.15625
- coupling_top: bfloat16 [8, 32, 16, 4, 64], P('gx', 'gy'), may hold values from -0.21875 to 0.21875
Outputs:
- first_product: float32 [8, 8, 32, 2048], P(None, 'gx', 'gy')
- second_product: float32 [8, 8, 32, 2048], P(None, 'gx', 'gy')
The draws below stay inside these ranges and needn't reach their ends.
Inputs may be any that keep to these rules, and one draw needn't show every extreme that they name: `point_slot`: every device's entries along the last dimension are a permutation of 0 to 2047.
All inputs are finite; a program needn't handle non-finite values.
Results may differ from the reference program's by a relative error of at most 0.025.
Values may be sent and summed in bfloat16 or wider, within the bound.
A program may use at most 128 MiB of HBM per device.

```python
import jax
import jax.numpy as jnp
import numpy as np

LEAF = 128
RANK = 64
SIDE = 4
RHS = 8
PDEV = 2048
R0 = 32
C0 = 128
TOPB = 16
N_GX = 8
N_GY = 32


def level_of(stream_key, extent, pieces, least, top_value):
    def one(position, parts):
        draws = jax.random.uniform(jax.random.fold_in(jax.random.fold_in(stream_key, 6), position), (parts,), jnp.float32, least / len(pieces), top_value / len(pieces))
        return jnp.repeat(jnp.exp(draws), extent[position] // parts).reshape((-1,) + (1,) * (len(extent) - position - 1))

    level = one(*pieces[0])
    for cut in pieces[1:]:
        level = level * one(*cut)
    return level


def normal_values(stream_key, shape, scale, reach, shards=(), kind=jnp.bfloat16):
    values = jax.random.normal(stream_key, shape, jnp.float32) * scale
    if len(shards) > 0:
        values = level_of(stream_key, shape, shards, -0.22, 0.18) * values
    return jnp.clip(values, min=-reach, max=reach).astype(kind)


def setup_inputs(seed: int = 0) -> dict:
    splits = jax.random.split(jax.random.key(seed), 14)
    values = normal_values(splits[0], (RHS, N_GX, N_GY, PDEV), 1.0, 6.0, ((1, 8), (2, 32)))
    point_slot = jax.vmap(lambda own: jax.random.permutation(own, PDEV))(jax.random.split(splits[1], N_GX * N_GY)).reshape((N_GX, N_GY, PDEV)).astype(jnp.int32)
    leaf_basis = normal_values(splits[2], (R0, C0, LEAF, RANK), LEAF ** -0.5, 0.5, ((0, 8), (1, 32)))
    near_blocks = normal_values(splits[3], (R0, C0, 9, LEAF, LEAF), (9 * LEAF) ** -0.5, 0.1875, ((0, 8), (1, 32)))
    transfer_leaf = normal_values(splits[4], (R0, C0, RANK, RANK), (2 * RANK) ** -0.5, 0.5, ((0, 8), (1, 32)))
    transfer_mid = normal_values(splits[5], (R0 // 2, C0 // 2, RANK, RANK), (2 * RANK) ** -0.5, 0.5, ((0, 8), (1, 32)))
    transfer_dev = normal_values(splits[6], (N_GX, N_GY, RANK, RANK), (2 * RANK) ** -0.5, 0.5, ((0, 8), (1, 32)))
    transfer_coarse = normal_values(splits[7], (N_GX // 2, N_GY // 2, RANK, RANK), (2 * RANK) ** -0.5, 0.5)
    coupling_leaf = normal_values(splits[8], (R0, C0, 36, RANK, RANK), (27 * RANK) ** -0.5, 0.15625, ((0, 8), (1, 32)))
    coupling_mid = normal_values(splits[9], (R0 // 2, C0 // 2, 36, RANK, RANK), (27 * RANK) ** -0.5, 0.15625, ((0, 8), (1, 32)))
    coupling_dev = normal_values(splits[10], (N_GX, N_GY, 36, RANK, RANK), (27 * RANK) ** -0.5, 0.15625, ((0, 8), (1, 32)))
    coupling_coarse = normal_values(splits[11], (N_GX, N_GY, 36, RANK // 4, RANK), (27 * RANK) ** -0.5, 0.15625, ((0, 8), (1, 32)))
    coupling_top = normal_values(splits[12], (N_GX, N_GY, TOPB, RANK // 16, RANK), (12 * RANK) ** -0.5, 0.21875, ((0, 8), (1, 32)))
    return dict(values=values, point_slot=point_slot, leaf_basis=leaf_basis, near_blocks=near_blocks, transfer_leaf=transfer_leaf, transfer_mid=transfer_mid, transfer_dev=transfer_dev, transfer_coarse=transfer_coarse, coupling_leaf=coupling_leaf, coupling_mid=coupling_mid, coupling_dev=coupling_dev, coupling_coarse=coupling_coarse, coupling_top=coupling_top)


def slot_table():
    mask_table = np.ones((2, 2, 36), np.float32)
    for row_bit in range(2):
        for col_bit in range(2):
            for slot_index in range(36):
                if abs(slot_index // 6 - 2 - row_bit) <= 1 and abs(slot_index % 6 - 2 - col_bit) <= 1:
                    mask_table[row_bit, col_bit, slot_index] = 0.0
    return mask_table


def index_arrays(point_slot, vectors):
    lead_index = jnp.arange(vectors).astype(jnp.int32)[:, None, None, None]
    grid_row = jnp.arange(N_GX).astype(jnp.int32)[None, :, None, None]
    grid_col = jnp.arange(N_GY).astype(jnp.int32)[None, None, :, None]
    return lead_index, grid_row, grid_col, point_slot[None].astype(jnp.int32)


def to_grid(values):
    vectors = values.shape[0]
    blocks = values.reshape(vectors, N_GX, N_GY, SIDE, SIDE, LEAF)
    return blocks.transpose(0, 1, 3, 2, 4, 5).reshape(vectors, N_GX * SIDE, N_GY * SIDE, LEAF)


def from_grid(leaf_field):
    vectors = leaf_field.shape[0]
    blocks = leaf_field.reshape(vectors, N_GX, SIDE, N_GY, SIDE, LEAF)
    return blocks.transpose(0, 1, 3, 2, 4, 5).reshape(vectors, N_GX, N_GY, SIDE * SIDE * LEAF)


def lift_level(coeffs, transfer):
    vectors, row_count, col_count, span_width = coeffs.shape
    child_terms = jnp.einsum('rijk,ijkm->rijm', coeffs.astype(jnp.float32), transfer.astype(jnp.float32))
    child_terms = child_terms.reshape(vectors, row_count // 2, 2, col_count // 2, 2, span_width)
    return child_terms.sum(axis=(2, 4)).astype(jnp.bfloat16)


def lower_level(parent, transfer):
    spread = jnp.repeat(jnp.repeat(parent, 2, axis=1), 2, axis=2)
    return jnp.einsum('ijkm,rijm->rijk', transfer.astype(jnp.float32), spread.astype(jnp.float32))


def far_whole(coeffs, coupling):
    vectors, row_count, col_count, span_width = coeffs.shape
    padded = jnp.pad(coeffs, ((0, 0), (2, 2), (2, 2), (0, 0)))
    keep_mask = jnp.asarray(np.tile(slot_table(), (row_count // 2, col_count // 2, 1)), coeffs.dtype)
    total = jnp.zeros((vectors, row_count, col_count, coupling.shape[3]), jnp.float32)
    for slot_index in range(36):
        row_first = slot_index // 6
        col_first = slot_index % 6
        source = padded[:, row_first:row_first + row_count:2, col_first:col_first + col_count:2]
        source = jnp.repeat(jnp.repeat(source, 2, axis=1), 2, axis=2)
        source = source * keep_mask[None, :, :, slot_index, None]
        total = total + jnp.einsum('rijk,ijmk->rijm', source.astype(jnp.float32),
                                   coupling[:, :, slot_index].astype(jnp.float32))
    return total


def third_level(coupling):
    row_count, col_count = N_GX // 2, N_GY // 2
    slot_count, part_rows, span_width = coupling.shape[2], coupling.shape[3], coupling.shape[4]
    blocks = coupling.reshape(row_count, 2, col_count, 2, slot_count, part_rows, span_width)
    return blocks.transpose(0, 2, 4, 1, 3, 5, 6).reshape(row_count, col_count, slot_count, 4 * part_rows, span_width)


def top_whole(coeffs, coupling):
    vectors, row_count, col_count, span_width = coeffs.shape
    box_count = row_count * col_count
    coupling = jnp.roll(coupling, N_GX // 2, axis=0)
    blocks = coupling.reshape(row_count, 2, 2, col_count, 2, 2, box_count, span_width // 16, span_width)
    blocks = blocks.transpose(0, 3, 6, 1, 4, 2, 5, 7, 8).reshape(row_count, col_count, box_count, span_width, span_width)
    target_row = jnp.arange(row_count).astype(jnp.int32)[:, None, None]
    target_col = jnp.arange(col_count).astype(jnp.int32)[None, :, None]
    source_box = jnp.arange(box_count).astype(jnp.int32)[None, None, :]
    far_enough = jnp.maximum(jnp.abs(source_box // col_count - target_row), jnp.abs(source_box % col_count - target_col)) >= 2
    weights = blocks.astype(jnp.float32) * far_enough[:, :, :, None, None].astype(jnp.float32)
    flat_coeffs = coeffs.reshape(vectors, box_count, span_width).astype(jnp.float32)
    return jnp.einsum('rtk,pqtmk->rpqm', flat_coeffs, weights)


def product(values, point_slot, leaf_basis, near_blocks, transfers, couplings):
    vectors = values.shape[0]
    lead_index, grid_row, grid_col, slot_index = index_arrays(point_slot, vectors)
    leaf_grid = to_grid(values[lead_index, grid_row, grid_col, slot_index])
    row_count, col_count = leaf_grid.shape[1], leaf_grid.shape[2]
    padded = jnp.pad(leaf_grid, ((0, 0), (1, 1), (1, 1), (0, 0)))
    near_part = jnp.zeros(leaf_grid.shape, jnp.float32)
    for near_index in range(9):
        row_first = near_index // 3
        col_first = near_index % 3
        window = padded[:, row_first:row_first + row_count, col_first:col_first + col_count]
        near_part = near_part + jnp.einsum('rijt,ijst->rijs', window.astype(jnp.float32),
                                           near_blocks[:, :, near_index].astype(jnp.float32))
    level_zero = jnp.einsum('rijs,ijsk->rijk', leaf_grid.astype(jnp.float32),
                            leaf_basis.astype(jnp.float32)).astype(jnp.bfloat16)
    levels = [level_zero]
    for transfer in transfers:
        levels.append(lift_level(levels[-1], transfer))
    far_fields = [far_whole(levels[0], couplings[0]), far_whole(levels[1], couplings[1]),
                  far_whole(levels[2], couplings[2]), far_whole(levels[3], third_level(couplings[3]))]
    local_field = top_whole(levels[4], couplings[4])
    for level_index in [3, 2, 1, 0]:
        local_field = far_fields[level_index] + lower_level(local_field.astype(jnp.bfloat16), transfers[level_index])
    far_part = jnp.einsum('ijsk,rijk->rijs', leaf_basis.astype(jnp.float32),
                          local_field.astype(jnp.bfloat16).astype(jnp.float32))
    ordered = from_grid(near_part + far_part)
    return jnp.zeros(ordered.shape, ordered.dtype).at[lead_index, grid_row, grid_col, slot_index].set(ordered)


def reference(values, point_slot, leaf_basis, near_blocks, transfer_leaf, transfer_mid, transfer_dev,
              transfer_coarse, coupling_leaf, coupling_mid, coupling_dev, coupling_coarse, coupling_top):
    transfers = [transfer_leaf, transfer_mid, transfer_dev, transfer_coarse]
    couplings = [coupling_leaf, coupling_mid, coupling_dev, coupling_coarse, coupling_top]
    first_product = product(values, point_slot, leaf_basis, near_blocks, transfers, couplings)
    second_product = product(first_product.astype(jnp.bfloat16), point_slot, leaf_basis, near_blocks,
                             transfers, couplings)
    return first_product, second_product
```

```python
import functools

import jax
import jax.numpy as jnp
from jax import lax
from jax.experimental import pallas as pl
from jax.experimental.pallas import tpu as pltpu
from jax.sharding import PartitionSpec as P

F32 = jnp.float32
BF16 = jnp.bfloat16
I32 = jnp.int32
MESH = pl.DeviceIdType.MESH
NN = (((1,), (0,)), ((), ()))
NT = (((1,), (1,)), ((), ()))
VMEM_LIMIT = 56 * 2**20

BLOCK_PEERS = [(a, b) for a in range(4) for b in range(4) if a or b]
TOP_PEERS = [(a, b) for b in (3, 5, 1, 7, 4, 2, 6) for a in (1, 0)] + [(1, 0)]
NEXT_TOP = [(1, 1), (1, -1), (1, 0), (0, 1), (0, -1)]
SIBLINGS = [(1, 0), (0, 1), (1, 1)]
BESIDE = [(a, b) for a in (-1, 0, 1) for b in (-1, 0, 1) if a or b]
LOCAL_ARRAYS = 10


def dot(left, right, dims):
    return lax.dot_general(left, right, dims, preferred_element_type=F32)


def permute(blocks, index_row):
    index = jnp.broadcast_to(index_row, (8, 128))
    lane = index & 127
    source = index >> 7
    result = None
    for block, piece in enumerate(blocks):
        taken = jnp.take_along_axis(piece, lane, axis=1, mode="promise_in_bounds")
        result = taken if result is None else jnp.where(source == block, taken, result)
    return result


def prepare_kernel(values_ref, slot_ref, top_ref, grid_ref, inverse_ref, part_ref, part_wide):
    values = jnp.concatenate([values_ref[r, 0].astype(F32) for r in range(8)], axis=0)
    pieces = [values[:, 128 * s : 128 * s + 128] for s in range(16)]
    for m in range(16):
        grid_ref[m] = permute(pieces, slot_ref[0, 0:1, 128 * m : 128 * m + 128])
    slots = slot_ref[0]
    position = lax.broadcasted_iota(I32, (16, 2048), 1)
    own_block = lax.broadcasted_iota(I32, (16, 2048), 0) == (slots >> 7)
    coded = jnp.concatenate(
        [
            jnp.where(own_block, (position >> 7).astype(F32), 0.0),
            jnp.where(own_block, (position & 127).astype(F32), 0.0),
        ],
        axis=0,
    ).astype(BF16)
    own_lane = lax.broadcasted_iota(I32, (128, 2048), 0) == (slots & 127)
    counted = dot(coded, jnp.where(own_lane, 1.0, 0.0).astype(BF16), NT)
    inverse_ref[...] = (counted[:16] * 128.0 + counted[16:]).astype(I32)
    for t in range(16):
        part_wide[4 * (t // 4) : 4 * (t // 4) + 4, 64 * (t % 4) : 64 * (t % 4) + 64] = top_ref[
            0, 0, t
        ].astype(F32)
    part_ref[...] = part_wide[...].astype(BF16)


def place_kernel(ordered_ref, inverse_ref, first_ref, second_ref):
    for which, placed_ref in enumerate((first_ref, second_ref)):
        pieces = [ordered_ref[which, s] for s in range(16)]
        for m in range(16):
            result = permute(pieces, inverse_ref[m : m + 1])
            for r in range(8):
                placed_ref[r, 0, 0:1, 128 * m : 128 * m + 128] = result[r : r + 1]


def keeps(slot, child):
    return abs(slot // 6 - 2 - child // 2) > 1 or abs(slot % 6 - 2 - child % 2) > 1


def far_children(pairs, weight):
    low = lax.broadcasted_iota(I32, (8, 128), 1) < 64
    zero = jnp.zeros((8, 128), F32)
    total = None
    for u in range(18):
        rows = []
        for child in range(4):
            first, second = keeps(u, child), keeps(u + 18, child)
            if first and second:
                rows.append(pairs[u])
            elif first:
                rows.append(jnp.where(low, pairs[u], zero))
            elif second:
                rows.append(jnp.where(low, zero, pairs[u]))
            else:
                rows.append(zero)
        sources = jnp.concatenate(rows, axis=0).astype(BF16)
        matrices = jnp.concatenate([weight(child, u) for child in range(4)], axis=0)
        term = dot(sources, matrices, NT)
        total = term if total is None else total + term
    owner = lax.broadcasted_iota(I32, (8, 256), 1) >> 6
    result = jnp.zeros((8, 256), F32)
    for child in range(4):
        result = result + jnp.where(owner == child, total[8 * child : 8 * child + 8], 0.0)
    return result


def window_mask(row, col, rows, cols):
    slot = lax.broadcasted_iota(I32, (8, 2304), 1) >> 6
    slot_row = (slot * 43) >> 8
    slot_col = slot - 6 * slot_row
    source_row = slot_row + 2 * (row // 2) - 2
    source_col = slot_col + 2 * (col // 2) - 2
    inside = (source_row >= 0) & (source_row < rows) & (source_col >= 0) & (source_col < cols)
    apart = (jnp.abs(source_row - row) > 1) | (jnp.abs(source_col - col) > 1)
    return jnp.where(inside & apart, 1.0, 0.0)


def strip(step):
    return {-1: (2, 6, 2), 0: (2, 2, 4), 1: (4, 0, 2)}[step]


def main_kernel(
    grid_rows,
    grid_cols,
    grid_ref,
    part_ref,
    basis_any,
    near_any,
    e0_any,
    e1_any,
    e2_any,
    e3_any,
    m0_any,
    m1_any,
    m2_any,
    m3_any,
    out_ref,
    basis,
    near,
    e0,
    e1,
    e2,
    e3,
    m0,
    m1,
    m2,
    m3,
    m0_pairs,
    m1_pairs,
    w2,
    w3,
    w4,
    e3_twice,
    e3_spread,
    mask2,
    mask3,
    mask4,
    halo,
    window,
    threes,
    fours,
    pair_tiles,
    near_sum,
    far_zero,
    far_one,
    local_sem,
    block_send,
    block_recv,
    top_send,
    top_recv,
    three_send,
    three_recv,
    side_send,
    side_recv,
    halo_send,
    halo_recv,
    w3_send,
    w3_recv,
    cross_send,
    cross_recv,
    w4_send,
    w4_recv,
):
    i = lax.axis_index("gx")
    j = lax.axis_index("gy")
    in_row, in_col = i % 4, j % 4
    half_row, half_col = in_row // 2, in_col // 2
    row_start, col_start = 2 - 2 * half_row, 2 - 2 * half_col
    own_top = (i // 4) * 8 + j // 4

    def block_peer(a, b):
        return (4 * (i // 4) + (in_row + a) % 4, 4 * (j // 4) + (in_col + b) % 4)

    def top_peer(a, b):
        return ((i + 4 * a) % grid_rows, (j + 4 * b + grid_cols) % grid_cols)

    def beside(a, b):
        return ((i + a + grid_rows) % grid_rows, (j + b + grid_cols) % grid_cols)

    def remote(source, target, send, recv, peer):
        return pltpu.make_async_remote_copy(
            src_ref=source,
            dst_ref=target,
            send_sem=send,
            recv_sem=recv,
            device_id=peer,
            device_id_type=MESH,
        )

    barrier = pltpu.get_barrier_semaphore()
    for a, b in TOP_PEERS:
        pl.semaphore_signal(barrier, 1, device_id=top_peer(a, b), device_id_type=MESH)
    for a, b in BLOCK_PEERS:
        pl.semaphore_signal(barrier, 1, device_id=block_peer(a, b), device_id_type=MESH)
    for a, b in BESIDE:
        pl.semaphore_signal(barrier, 1, device_id=beside(a, b), device_id_type=MESH)

    e3_own = e3_any.at[pl.ds(2 * (i // 4), 2), pl.ds(2 * (j // 4), 2)]
    staged = [
        (basis_any, basis),
        (e0_any, e0),
        (e1_any, e1),
        (e2_any, e2),
        (m3_any, m3),
        (m2_any, m2),
        (e3_own, e3),
        (m1_any, m1),
        (m0_any, m0),
        (near_any, near),
    ]
    loads = [
        pltpu.make_async_copy(source, target, local_sem.at[n])
        for n, (source, target) in enumerate(staged)
    ]
    for load in loads:
        load.start()

    low = lax.broadcasted_iota(I32, (8, 128), 1) < 64

    def up(product, leaf):
        level_zero = [
            dot(leaf[n].astype(BF16), basis[n // 4, n % 4], NN) for n in range(16)
        ]
        level_one = []
        for p in range(4):
            pa, pb = p // 2, p % 2
            children = jnp.concatenate(
                [level_zero[4 * (2 * pa + c // 2) + 2 * pb + c % 2] for c in range(4)], axis=1
            ).astype(BF16)
            transfer = e0[2 * pa : 2 * pa + 2, 2 * pb : 2 * pb + 2].reshape(256, 64)
            level_one.append(dot(children, transfer, NN))
        children = jnp.concatenate(level_one, axis=1).astype(BF16)
        level_two = dot(children, e1[...].reshape(256, 64), NN)
        term = dot(level_two.astype(BF16), e2[0, 0], NN)
        window[product, row_start + in_row, col_start + in_col] = jnp.concatenate(
            [term, level_two], axis=1
        )
        for n in range(16):
            a, b = n // 4, n % 4
            coeffs = jnp.concatenate(
                [level_zero[n], level_one[2 * (a % 2) + b % 2]], axis=1
            )
            halo[product, 2 + a, 2 + b] = jnp.concatenate([leaf[n], coeffs], axis=0).astype(BF16)

    for n in range(4):
        loads[n].wait()
    up(0, [grid_ref[n] for n in range(16)])

    own_three = 2 * (i % 2) + j % 2
    own_four = 8 * half_row + 4 * half_col + own_three
    loads[4].wait()
    for u in range(18):
        w3[own_three, :, 128 * u : 128 * u + 128] = jnp.concatenate(
            [m3[0, 0, 2 * u], m3[0, 0, 2 * u + 1]], axis=1
        )
    loads[5].wait()
    for u in range(18):
        w2[:, 128 * u : 128 * u + 128] = jnp.concatenate(
            [m2[0, 0, 2 * u], m2[0, 0, 2 * u + 1]], axis=1
        )
    loads[6].wait()
    coarse = e3[...].reshape(256, 64)
    e3_twice[...] = jnp.concatenate([coarse, coarse], axis=1)
    spread_row = lax.broadcasted_iota(I32, (256, 64), 0)
    spread_col = lax.broadcasted_iota(I32, (256, 64), 1)
    chosen = spread_col == (spread_row >> 4) * 4 + (spread_row & 3)
    e3_spread[...] = dot(
        jnp.where(chosen, 1.0, 0.0).astype(BF16), e3[half_row, half_col], NT
    ).astype(BF16)
    mask2[...] = window_mask(i, j, grid_rows, grid_cols)
    mask3[...] = window_mask(i // 2, j // 2, grid_rows // 2, grid_cols // 2)
    quarter = lax.broadcasted_iota(I32, (32, 256), 0) >> 3
    top_box = 4 * quarter + (lax.broadcasted_iota(I32, (32, 256), 1) >> 6)
    apart = (jnp.abs((top_box >> 3) - i // 4) > 1) | (jnp.abs((top_box & 7) - j // 4) > 1)
    mask4[...] = jnp.where(apart, 1.0, 0.0)

    def w3_copies():
        return [
            remote(
                w3.at[own_three],
                w3.at[own_three],
                w3_send.at[n],
                w3_recv.at[n],
                (2 * (i // 2) + (i + a) % 2, 2 * (j // 2) + (j + b) % 2),
            )
            for n, (a, b) in enumerate(SIBLINGS)
        ]

    def cross_copy():
        return remote(
            part_ref, w4.at[own_four], cross_send.at[0], cross_recv.at[0], top_peer(1, 0)
        )

    def w4_copies():
        return [
            remote(
                w4.at[own_four], w4.at[own_four], w4_send.at[n], w4_recv.at[n], block_peer(a, b)
            )
            for n, (a, b) in enumerate(BLOCK_PEERS)
        ]

    def top_copies(product):
        return [
            remote(
                fours.at[product, own_top],
                fours.at[product, own_top],
                top_send.at[product, n],
                top_recv.at[product, n],
                top_peer(a, b),
            )
            for n, (a, b) in enumerate(TOP_PEERS)
        ]

    pl.semaphore_wait(barrier, len(TOP_PEERS) + len(BLOCK_PEERS) + len(BESIDE))

    def apply(product, carry):
        block_copies = []
        for n, (a, b) in enumerate(BLOCK_PEERS):
            peer_row, peer_col = block_peer(a, b)
            target_row = in_row + 2 - 2 * ((peer_row % 4) // 2)
            target_col = in_col + 2 - 2 * ((peer_col % 4) // 2)
            block_copies.append(
                remote(
                    window.at[product, row_start + in_row, col_start + in_col],
                    window.at[product, target_row, target_col],
                    block_send.at[product, n],
                    block_recv.at[product, n],
                    (peer_row, peer_col),
                )
            )
        halo_copies = []
        for n, (a, b) in enumerate(BESIDE):
            row_from, row_to, row_count = strip(a)
            col_from, col_to, col_count = strip(b)
            halo_copies.append(
                remote(
                    halo.at[product, pl.ds(row_from, row_count), pl.ds(col_from, col_count)],
                    halo.at[product, pl.ds(row_to, row_count), pl.ds(col_to, col_count)],
                    halo_send.at[product, n],
                    halo_recv.at[product, n],
                    beside(a, b),
                )
            )
        for copy in block_copies:
            copy.start()
        for copy in halo_copies:
            copy.start()

        @pl.when(product == 0)
        def _():
            cross_copy().start()
            for copy in w3_copies():
                copy.start()
            loads[7].wait()
            for n in range(4):
                for u in range(18):
                    m1_pairs[n, u] = jnp.concatenate(
                        [m1[n // 2, n % 2, u], m1[n // 2, n % 2, u + 18]], axis=1
                    )
            loads[8].wait()

            def pack(n, inner):
                for u in range(18):
                    m0_pairs[n, u] = jnp.concatenate(
                        [m0[n // 4, n % 4, u], m0[n // 4, n % 4, u + 18]], axis=1
                    )
                return inner

            lax.fori_loop(0, 16, pack, 0)
            loads[9].wait()

        for copy in block_copies:
            copy.wait_recv()
        rows = []
        for a in range(2):
            sums = []
            for b in range(2):
                total = None
                for c in range(4):
                    tile = window[
                        product,
                        row_start + 2 * a + c // 2,
                        col_start + 2 * b + c % 2,
                    ]
                    total = tile if total is None else total + tile
                sums.append(total)
            rows.append(jnp.where(low, sums[0], pltpu.roll(sums[1], 64, 1)))
        threes[product, 0, 1] = jnp.concatenate(rows, axis=0).astype(BF16)
        fours[product, own_top] = dot(
            jnp.concatenate(rows, axis=1).astype(BF16), e3_twice[...], NN
        )
        for copy in top_copies(product):
            copy.start()
        three_copies = [
            remote(
                threes.at[product, 0, 1],
                threes.at[product, a, 1 - b],
                three_send.at[product, n],
                three_recv.at[product, n],
                top_peer(a, b),
            )
            for n, (a, b) in enumerate(NEXT_TOP)
        ]
        for copy in three_copies:
            copy.start()
        row_from, row_to = 4 - 4 * half_row, 4 * half_row
        col_from, col_to = 4 - 4 * half_col, 4 * half_col
        side_col = 1 - 2 * half_col
        side_copies = []
        for n, (a, b) in enumerate(SIBLINGS):
            source_rows = pl.ds(row_from, 2) if a else pl.ds(row_start, 4)
            target_rows = pl.ds(row_to, 2) if a else pl.ds(row_start, 4)
            source_cols = pl.ds(col_from, 2) if b else pl.ds(col_start, 4)
            target_cols = pl.ds(col_to, 2) if b else pl.ds(col_start, 4)
            side_copies.append(
                remote(
                    window.at[product, source_rows, source_cols],
                    window.at[product, target_rows, target_cols],
                    side_send.at[product, n],
                    side_recv.at[product, n],
                    top_peer(a, b * side_col),
                )
            )
        for copy in side_copies:
            copy.start()

        @pl.when(product == 0)
        def _():
            cross_copy().wait_recv()
            for copy in w4_copies():
                copy.start()

        for copy in halo_copies:
            copy.wait_recv()
        blank = jnp.zeros((16, 128), BF16)

        def clear(cells):
            for a, b in cells:
                halo[product, a, b] = blank

        @pl.when(i == 0)
        def _():
            clear([(a, b) for a in (0, 1) for b in range(8)])

        @pl.when(i == grid_rows - 1)
        def _():
            clear([(a, b) for a in (6, 7) for b in range(8)])

        @pl.when(j == 0)
        def _():
            clear([(a, b) for a in range(8) for b in (0, 1)])

        @pl.when(j == grid_cols - 1)
        def _():
            clear([(a, b) for a in range(8) for b in (6, 7)])

        def near_row(a, inner):
            for b in range(4):
                total = None
                for n in range(9):
                    source = halo[product, a + 1 + n // 3, b + 1 + n % 3].astype(F32)
                    term = dot(source[:8].astype(BF16), near[a, b, n], NT)
                    total = term if total is None else total + term
                near_sum[4 * a + b] = total
            return inner

        lax.fori_loop(0, 4, near_row, 0)

        def coeffs(a, b):
            return halo[product, a, b].astype(F32)[8:]

        for b in range(8):
            column = [coeffs(a, b) for a in range(8)]
            for a in range(5):
                pair_tiles[a, b] = jnp.where(low, column[a], pltpu.roll(column[a + 3], 64, 1))

        def far_parent(p, inner):
            pa, pb = p // 2, p % 2
            pairs = [pair_tiles[2 * pa + u // 6, 2 * pb + u % 6] for u in range(18)]
            far_zero[p] = far_children(
                pairs,
                lambda child, u: m0_pairs[
                    4 * (2 * pa + child // 2) + 2 * pb + child % 2, u
                ],
            )
            return inner

        lax.fori_loop(0, 4, far_parent, 0)
        place = (0, 1, 2, 3, 6, 7)
        one_pairs = [
            jnp.where(
                low,
                pltpu.roll(coeffs(place[u // 6], place[u % 6]), 64, 1),
                coeffs(place[u // 6 + 3], place[u % 6]),
            )
            for u in range(18)
        ]
        far_one[...] = far_children(one_pairs, lambda child, u: m1_pairs[child, u])

        for copy in side_copies:
            copy.wait_recv()
        two_sources = []
        for u in range(18):
            first = window[product, u // 3, 2 * (u % 3)]
            second = window[product, u // 3, 2 * (u % 3) + 1]
            two_sources.append(jnp.where(low, pltpu.roll(first, 64, 1), second))
        two_sources = jnp.where(mask2[...] > 0.0, jnp.concatenate(two_sources, axis=1), 0.0)
        far_two = dot(two_sources.astype(BF16), w2[...], NT)

        @pl.when(product == 0)
        def _():
            for copy in w3_copies():
                copy.wait_recv()

        for copy in three_copies:
            copy.wait_recv()
        three_tiles = [
            [threes[product, a, b].astype(F32) for b in range(3)] for a in range(2)
        ]
        three_sources = jnp.concatenate(
            [
                three_tiles[0 if u // 6 == 1 else 1][u % 3][8 * ((u // 3) % 2) :][:8]
                for u in range(18)
            ],
            axis=1,
        )
        three_sources = jnp.where(mask3[...] > 0.0, three_sources, 0.0)
        far_three = dot(three_sources.astype(BF16), w3[...].reshape(64, 2304), NT)

        for copy in block_copies + halo_copies + three_copies + side_copies:
            copy.wait_send()

        @pl.when(product == 0)
        def _():
            for copy in w4_copies():
                copy.wait_recv()

        for copy in top_copies(product):
            copy.wait_recv()
        quarters = []
        for q in range(4):
            tiles = [fours[product, 4 * q + t] for t in range(4)]
            quarters.append(
                jnp.concatenate(
                    [jnp.where(low, tiles[0], tiles[1]), jnp.where(low, tiles[2], tiles[3])],
                    axis=1,
                )
            )
        four_sources = jnp.where(mask4[...] > 0.0, jnp.concatenate(quarters, axis=0), 0.0)
        crossed = dot(four_sources.astype(BF16), w4[...].reshape(256, 256), NT)
        lane_quarter = (lax.broadcasted_iota(I32, (8, 256), 1) >> 2) & 3
        far_four = jnp.zeros((8, 256), F32)
        for q in range(4):
            far_four = far_four + jnp.where(lane_quarter == q, crossed[8 * q : 8 * q + 8], 0.0)

        local_three = far_three + dot(far_four.astype(BF16), e3_spread[...], NN)
        local_two = far_two + dot(local_three.astype(BF16), e2[0, 0], NT)
        local_one = far_one[...] + dot(local_two.astype(BF16), e1[...].reshape(256, 64), NT)
        results = [None] * 16
        for p in range(4):
            pa, pb = p // 2, p % 2
            transfer = e0[2 * pa : 2 * pa + 2, 2 * pb : 2 * pb + 2].reshape(256, 64)
            local_zero = far_zero[p] + dot(
                local_one[:, 64 * p : 64 * p + 64].astype(BF16), transfer, NT
            )
            for c in range(4):
                a, b = 2 * pa + c // 2, 2 * pb + c % 2
                results[4 * a + b] = near_sum[4 * a + b] + dot(
                    local_zero[:, 64 * c : 64 * c + 64].astype(BF16), basis[a, b], NT
                )
        for n in range(16):
            out_ref[product, n] = results[n]

        @pl.when(product == 0)
        def _():
            up(1, results)

        return carry

    lax.fori_loop(0, 2, apply, 0)
    for product in range(2):
        for copy in top_copies(product):
            copy.wait_send()
    cross_copy().wait_send()
    for copy in w3_copies() + w4_copies():
        copy.wait_send()


def local(
    grid_rows,
    grid_cols,
    values,
    point_slot,
    leaf_basis,
    near_blocks,
    transfer_leaf,
    transfer_mid,
    transfer_dev,
    transfer_coarse,
    coupling_leaf,
    coupling_mid,
    coupling_dev,
    coupling_coarse,
    coupling_top,
):
    whole = pl.BlockSpec(memory_space=pltpu.VMEM)
    left = pl.BlockSpec(memory_space=pl.ANY)
    dma = pltpu.SemaphoreType.DMA
    params = pltpu.CompilerParams(vmem_limit_bytes=VMEM_LIMIT)
    ordered, inverse, part = pl.pallas_call(
        prepare_kernel,
        out_shape=(
            jax.ShapeDtypeStruct((16, 8, 128), F32),
            jax.ShapeDtypeStruct((16, 128), I32),
            jax.ShapeDtypeStruct((16, 256), BF16),
        ),
        in_specs=[whole] * 3,
        out_specs=(whole,) * 3,
        scratch_shapes=[pltpu.VMEM((16, 256), F32)],
        compiler_params=params,
    )(values, point_slot, coupling_top)
    products = pl.pallas_call(
        functools.partial(main_kernel, grid_rows, grid_cols),
        out_shape=jax.ShapeDtypeStruct((2, 16, 8, 128), F32),
        in_specs=[whole, whole] + [left] * LOCAL_ARRAYS,
        out_specs=whole,
        scratch_shapes=[
            pltpu.VMEM((4, 4, 128, 64), BF16),
            pltpu.VMEM((4, 4, 9, 128, 128), BF16),
            pltpu.VMEM((4, 4, 64, 64), BF16),
            pltpu.VMEM((2, 2, 64, 64), BF16),
            pltpu.VMEM((1, 1, 64, 64), BF16),
            pltpu.VMEM((2, 2, 64, 64), BF16),
            pltpu.VMEM((4, 4, 36, 64, 64), BF16),
            pltpu.VMEM((2, 2, 36, 64, 64), BF16),
            pltpu.VMEM((1, 1, 36, 64, 64), BF16),
            pltpu.VMEM((1, 1, 36, 16, 64), BF16),
            pltpu.VMEM((16, 18, 64, 128), BF16),
            pltpu.VMEM((4, 18, 64, 128), BF16),
            pltpu.VMEM((64, 2304), BF16),
            pltpu.VMEM((4, 16, 2304), BF16),
            pltpu.VMEM((16, 16, 256), BF16),
            pltpu.VMEM((256, 128), BF16),
            pltpu.VMEM((256, 64), BF16),
            pltpu.VMEM((8, 2304), F32),
            pltpu.VMEM((8, 2304), F32),
            pltpu.VMEM((32, 256), F32),
            pltpu.VMEM((2, 8, 8, 16, 128), BF16),
            pltpu.VMEM((2, 6, 6, 8, 128), F32),
            pltpu.VMEM((2, 2, 3, 16, 128), BF16),
            pltpu.VMEM((2, 16, 8, 128), F32),
            pltpu.VMEM((5, 8, 8, 128), F32),
            pltpu.VMEM((16, 8, 128), F32),
            pltpu.VMEM((4, 8, 256), F32),
            pltpu.VMEM((8, 256), F32),
            dma((LOCAL_ARRAYS,)),
            dma((2, 15)),
            dma((2, 15)),
            dma((2, 15)),
            dma((2, 15)),
            dma((2, 5)),
            dma((2, 5)),
            dma((2, 3)),
            dma((2, 3)),
            dma((2, 8)),
            dma((2, 8)),
            dma((3,)),
            dma((3,)),
            dma((1,)),
            dma((1,)),
            dma((15,)),
            dma((15,)),
        ],
        compiler_params=pltpu.CompilerParams(
            collective_id=0, has_side_effects=True, vmem_limit_bytes=VMEM_LIMIT
        ),
    )(
        ordered,
        part,
        leaf_basis,
        near_blocks,
        transfer_leaf,
        transfer_mid,
        transfer_dev,
        transfer_coarse,
        coupling_leaf,
        coupling_mid,
        coupling_dev,
        coupling_coarse,
    )
    placed = jax.ShapeDtypeStruct(values.shape, F32)
    return pl.pallas_call(
        place_kernel,
        out_shape=(placed, placed),
        in_specs=[whole] * 2,
        out_specs=(whole,) * 2,
        compiler_params=params,
    )(products, inverse)


def solution(mesh):
    placed = (
        P(None, "gx", "gy", None),
        P("gx", "gy", None),
        P("gx", "gy", None, None),
        P("gx", "gy", None, None, None),
        P("gx", "gy", None, None),
        P("gx", "gy", None, None),
        P("gx", "gy", None, None),
        P(),
        P("gx", "gy", None, None, None),
        P("gx", "gy", None, None, None),
        P("gx", "gy", None, None, None),
        P("gx", "gy", None, None, None),
        P("gx", "gy", None, None, None),
    )
    return jax.shard_map(
        functools.partial(local, mesh.shape["gx"], mesh.shape["gy"]),
        mesh=mesh,
        in_specs=placed,
        out_specs=(P(None, "gx", "gy", None), P(None, "gx", "gy", None)),
        check_vma=False,
    )
```

```python
import functools

import jax
import jax.numpy as jnp
from jax import lax
from jax.experimental import pallas as pl
from jax.experimental.pallas import tpu as pltpu
from jax.sharding import PartitionSpec as P

F32 = jnp.float32
BF16 = jnp.bfloat16
I32 = jnp.int32
MESH = pl.DeviceIdType.MESH
NN = (((1,), (0,)), ((), ()))
NT = (((1,), (1,)), ((), ()))
VMEM_LIMIT = 56 * 2**20

BLOCK_PEERS = [(a, b) for b in (4, 3, 5, 2, 6, 1, 7) for a in (1, 0)] + [(1, 0)]
TOP_PEERS = [(2, 2), (2, 1), (2, 3), (1, 2), (3, 2), (1, 1), (1, 3), (3, 1), (3, 3)] + [
    (2, 0),
    (0, 2),
    (1, 0),
    (3, 0),
    (0, 1),
    (0, 3),
]
HALF_PEERS = [(a, b) for a in range(2) for b in range(4) if a or b]
BESIDE = [(a, b) for a in (-1, 0, 1) for b in (-1, 0, 1) if a or b]
LOCAL_ARRAYS = 10


def dot(left, right, dims):
    return lax.dot_general(left, right, dims, preferred_element_type=F32)


def permute(blocks, index_row):
    index = jnp.broadcast_to(index_row, (8, 128))
    lane = index & 127
    source = index >> 7
    result = None
    for block, piece in enumerate(blocks):
        taken = jnp.take_along_axis(piece, lane, axis=1, mode="promise_in_bounds")
        result = taken if result is None else jnp.where(source == block, taken, result)
    return result


def place_kernel(ordered_ref, inverse_ref, first_ref, second_ref):
    for which, placed_ref in enumerate((first_ref, second_ref)):
        pieces = [ordered_ref[which, s] for s in range(16)]
        for m in range(16):
            result = permute(pieces, inverse_ref[m : m + 1])
            for r in range(8):
                placed_ref[r, 0, 0:1, 128 * m : 128 * m + 128] = result[r : r + 1]


def keeps(slot, child):
    return abs(slot // 6 - 2 - child // 2) > 1 or abs(slot % 6 - 2 - child % 2) > 1


def far_children(pairs, weight):
    low = lax.broadcasted_iota(I32, (8, 128), 1) < 64
    zero = jnp.zeros((8, 128), F32)
    sources, matrices = [], []
    for u in range(18):
        rows = []
        for child in range(4):
            first, second = keeps(u, child), keeps(u + 18, child)
            if first and second:
                rows.append(pairs[u])
            elif first:
                rows.append(jnp.where(low, pairs[u], zero))
            elif second:
                rows.append(jnp.where(low, zero, pairs[u]))
            else:
                rows.append(zero)
        sources.append(jnp.concatenate(rows, axis=0).astype(BF16))
        matrices.append(jnp.concatenate([weight(child, u) for child in range(4)], axis=0))
    total = dot(jnp.concatenate(sources, axis=1), jnp.concatenate(matrices, axis=1), NT)
    owner = lax.broadcasted_iota(I32, (8, 256), 1) >> 6
    result = jnp.zeros((8, 256), F32)
    for child in range(4):
        result = result + jnp.where(owner == child, total[8 * child : 8 * child + 8], 0.0)
    return result


def window_mask(row, col, rows, cols):
    slot = lax.broadcasted_iota(I32, (8, 2304), 1) >> 6
    slot_row = (slot * 43) >> 8
    slot_col = slot - 6 * slot_row
    source_row = slot_row + 2 * (row // 2) - 2
    source_col = slot_col + 2 * (col // 2) - 2
    inside = (source_row >= 0) & (source_row < rows) & (source_col >= 0) & (source_col < cols)
    apart = (jnp.abs(source_row - row) > 1) | (jnp.abs(source_col - col) > 1)
    return jnp.where(inside & apart, 1.0, 0.0)


def strip(step):
    return {-1: (2, 6, 2), 0: (2, 2, 4), 1: (4, 0, 2)}[step]


def main_kernel(
    grid_rows,
    grid_cols,
    values_ref,
    slot_ref,
    top_ref,
    basis_any,
    near_any,
    e0_any,
    e1_any,
    e2_any,
    e3_any,
    m0_any,
    m1_any,
    m2_any,
    m3_any,
    out_ref,
    inverse_ref,
    basis,
    near,
    e0,
    e1,
    e2,
    e3,
    m0,
    m1,
    m2,
    m3,
    m0_pairs,
    m1_pairs,
    w2,
    w3,
    w4,
    part_wide,
    part,
    e3_twice,
    e3_spread,
    top_matrix,
    rise,
    fall,
    turn,
    lane_hot,
    mask2,
    mask3,
    mask4,
    halo,
    window,
    threes,
    fours,
    pair_tiles,
    near_sum,
    far_zero,
    local_sem,
    block_send,
    block_recv,
    top_send,
    top_recv,
    three_send,
    three_recv,
    side_send,
    side_recv,
    halo_send,
    halo_recv,
    w3_send,
    w3_recv,
    cross_send,
    cross_recv,
    w4_send,
    w4_recv,
):
    i = lax.axis_index("gx")
    j = lax.axis_index("gy")
    pair_row, core = i // 2, i % 2
    patch, depth = j // 8, j % 8
    half = depth // 4
    own_pair = depth // 2

    def block_peer(a, b):
        return (2 * pair_row + (core + a) % 2, 8 * patch + (depth + b) % 8)

    def half_peer(a, b):
        return (2 * pair_row + (core + a) % 2, 8 * patch + 4 * half + (depth + b) % 4)

    def top_peer(a, b):
        return ((i + 2 * a) % grid_rows, (j + 8 * b + grid_cols) % grid_cols)

    def beside(a, b):
        return ((i + a + grid_rows) % grid_rows, (j + b + grid_cols) % grid_cols)

    def remote(source, target, send, recv, peer):
        return pltpu.make_async_remote_copy(
            src_ref=source,
            dst_ref=target,
            send_sem=send,
            recv_sem=recv,
            device_id=peer,
            device_id_type=MESH,
        )

    barrier = pltpu.get_barrier_semaphore()
    for a, b in TOP_PEERS:
        pl.semaphore_signal(barrier, 1, device_id=top_peer(a, b), device_id_type=MESH)
    for a, b in BLOCK_PEERS:
        pl.semaphore_signal(barrier, 1, device_id=block_peer(a, b), device_id_type=MESH)
    for a, b in BESIDE:
        pl.semaphore_signal(barrier, 1, device_id=beside(a, b), device_id_type=MESH)

    e3_own = e3_any.at[pl.ds(pair_row, 1), pl.ds(4 * patch, 4)]
    staged = [
        (basis_any, basis),
        (e0_any, e0),
        (e1_any, e1),
        (e2_any, e2),
        (m3_any, m3),
        (m2_any, m2),
        (e3_own, e3),
        (m1_any, m1),
        (m0_any, m0),
        (near_any, near),
    ]
    loads = [
        pltpu.make_async_copy(source, target, local_sem.at[n])
        for n, (source, target) in enumerate(staged)
    ]
    for load in loads:
        load.start()

    low = lax.broadcasted_iota(I32, (8, 128), 1) < 64

    def coefficients(product, leaf):
        level_zero = [dot(leaf[n].astype(BF16), basis[n // 4, n % 4], NT) for n in range(16)]
        level_one = []
        for p in range(4):
            pa, pb = p // 2, p % 2
            children = jnp.concatenate(
                [level_zero[4 * (2 * pa + c // 2) + 2 * pb + c % 2] for c in range(4)], axis=1
            ).astype(BF16)
            transfer = e0[2 * pa : 2 * pa + 2, 2 * pb : 2 * pb + 2].reshape(256, 64)
            level_one.append(dot(children, transfer, NN))
        for n in range(16):
            a, b = n // 4, n % 4
            coeffs = jnp.concatenate(
                [level_zero[n], level_one[2 * (a % 2) + b % 2]], axis=1
            )
            halo[product, 2 + a, 2 + b] = jnp.concatenate([leaf[n], coeffs], axis=0).astype(BF16)
        return level_one

    slots = slot_ref[0]
    slot_lane = lax.broadcasted_iota(I32, (128, 2048), 0) == (slots & 127)
    lane_hot[...] = jnp.where(slot_lane, 1.0, 0.0).astype(BF16)
    values = values_ref[0, 0].astype(F32)
    stacked = jnp.concatenate([values[:, 128 * s : 128 * s + 128] for s in range(16)], axis=0)
    candidates = dot(stacked.astype(BF16), lane_hot[...], NN)
    slot_block = jnp.broadcast_to(slots >> 7, (8, 2048))
    ordered = jnp.zeros((8, 2048), F32)
    for s in range(16):
        ordered = jnp.where(slot_block == s, candidates[8 * s : 8 * s + 8], ordered)

    for n in range(4):
        loads[n].wait()
    level_one = coefficients(0, [ordered[:, 128 * n : 128 * n + 128] for n in range(16)])
    level_two = dot(
        jnp.concatenate(level_one, axis=1).astype(BF16), e1[...].reshape(256, 64), NN
    )
    term = dot(level_two.astype(BF16), e2[0, 0], NN)
    window[0, 1, core, 2 + depth] = jnp.concatenate(
        [term, level_two], axis=1
    )

    def block_copies(product):
        copies = []
        for n, (a, b) in enumerate(BLOCK_PEERS):
            copies.append(
                remote(
                    window.at[product, 1, core, 2 + depth],
                    window.at[product, 1, core, 2 + depth],
                    block_send.at[product, n],
                    block_recv.at[product, n],
                    block_peer(a, b),
                )
            )
        return copies

    def halo_copies(product):
        copies = []
        for n, (a, b) in enumerate(BESIDE):
            row_from, row_to, row_count = strip(a)
            col_from, col_to, col_count = strip(b)
            copies.append(
                remote(
                    halo.at[product, pl.ds(row_from, row_count), pl.ds(col_from, col_count)],
                    halo.at[product, pl.ds(row_to, row_count), pl.ds(col_to, col_count)],
                    halo_send.at[product, n],
                    halo_recv.at[product, n],
                    beside(a, b),
                )
            )
        return copies

    own_three = 2 * (i % 2) + j % 2
    own_four = 8 * (pair_row % 2) + 4 * (own_pair % 2) + own_three
    other_four = 8 - 8 * (pair_row % 2) + 4 * (own_pair % 2) + own_three
    next_three = 2 * (i % 2) + 1 - j % 2
    three_peers = [
        (2 * (i // 2) + (i + a) % 2, 2 * (j // 2) + (j + b) % 2) for a, b in ((1, 0), (0, 1))
    ]

    def w3_copy(n):
        return remote(
            w3.at[own_three], w3.at[own_three], w3_send.at[n], w3_recv.at[n], three_peers[n]
        )

    def w3_forward():
        return remote(
            w3.at[next_three], w3.at[next_three], w3_send.at[2], w3_recv.at[2], three_peers[0]
        )

    def cross_copies():
        return [
            remote(
                part, w4.at[own_four], cross_send.at[n], cross_recv.at[n], top_peer(a, 0)
            )
            for n, a in enumerate((2, 3 - 2 * (pair_row % 2)))
        ]

    def w4_copies():
        return [
            remote(
                w4.at[which],
                w4.at[which],
                w4_send.at[7 * m + n],
                w4_recv.at[7 * m + n],
                half_peer(a, b),
            )
            for m, which in enumerate((own_four, other_four))
            for n, (a, b) in enumerate(HALF_PEERS)
        ]

    def top_copies(product):
        return [
            remote(
                fours.at[product, pair_row, patch],
                fours.at[product, pair_row, patch],
                top_send.at[product, n],
                top_recv.at[product, n],
                top_peer(a, b),
            )
            for n, (a, b) in enumerate(TOP_PEERS)
        ]

    for t in range(16):
        part_wide[4 * (t // 4) : 4 * (t // 4) + 4, 64 * (t % 4) : 64 * (t % 4) + 64] = top_ref[
            0, 0, t
        ].astype(F32)
    part[...] = part_wide[...].astype(BF16)
    loads[4].wait()
    for u in range(18):
        w3[own_three, :, 128 * u : 128 * u + 128] = jnp.concatenate(
            [m3[0, 0, 2 * u], m3[0, 0, 2 * u + 1]], axis=1
        )
    loads[6].wait()
    coarse = e3[...].reshape(256, 64)
    first_half = lax.broadcasted_iota(I32, (256, 64), 0) < 128
    nothing = jnp.zeros((256, 64), F32)
    coarse = coarse.astype(F32)
    e3_twice[...] = jnp.concatenate(
        [jnp.where(first_half, coarse, nothing), jnp.where(first_half, nothing, coarse)], axis=1
    ).astype(BF16)
    loads[5].wait()

    pl.semaphore_wait(barrier, len(TOP_PEERS) + len(BLOCK_PEERS) + len(BESIDE))
    for copy in block_copies(0):
        copy.start()
    for copy in halo_copies(0):
        copy.start()

    def set_up():
        for copy in cross_copies():
            copy.start()
        loads[7].wait()
        for n in range(4):
            for u in range(18):
                m1_pairs[n, u] = jnp.concatenate(
                    [m1[n // 2, n % 2, u], m1[n // 2, n % 2, u + 18]], axis=1
                )
        loads[8].wait()

        def pack(n, inner):
            for u in range(18):
                m0_pairs[n, u] = jnp.concatenate(
                    [m0[n // 4, n % 4, u], m0[n // 4, n % 4, u + 18]], axis=1
                )
            return inner

        lax.fori_loop(0, 16, pack, 0)
        loads[9].wait()

    def set_up_more():
        for u in range(18):
            w2[:, 128 * u : 128 * u + 128] = jnp.concatenate(
                [m2[0, 0, 2 * u], m2[0, 0, 2 * u + 1]], axis=1
            )
        mask2[...] = window_mask(i, j, grid_rows, grid_cols)
        mask3[...] = window_mask(i // 2, j // 2, grid_rows // 2, grid_cols // 2)
        top_box = lax.broadcasted_iota(I32, (8, 1024), 1) >> 6
        apart = (jnp.abs((top_box >> 3) - i // 4) > 1) | (jnp.abs((top_box & 7) - j // 4) > 1)
        mask4[...] = jnp.where(apart, 1.0, 0.0)
        spread_row = lax.broadcasted_iota(I32, (64, 256), 0)
        spread_col = lax.broadcasted_iota(I32, (64, 256), 1)
        chosen = spread_row == (spread_col >> 4) * 4 + (spread_col & 3)
        spread = dot(e3[0, own_pair], jnp.where(chosen, 1.0, 0.0).astype(BF16), NN)
        for q in range(4):
            e3_spread[q] = jnp.where(((spread_col >> 2) & 3) == q, spread, 0.0).astype(BF16)
        total = None
        for n in range(16):
            a, b = n // 4, n % 4
            two = dot(e0[a, b], e1[a // 2, b // 2], NN)
            both = jnp.concatenate([dot(two.astype(BF16), e2[0, 0], NN), two], axis=1)
            up = dot(basis[a, b].astype(F32).T.astype(BF16), both.astype(BF16), NN)
            rise[n] = up.astype(BF16)
            fall[:, 128 * n : 128 * n + 128] = up.T.astype(BF16)
            around = dot(up.T.astype(BF16), up.astype(BF16), NN)
            total = around if total is None else total + around
        turn[...] = total.astype(BF16)
        slot_hot = lax.broadcasted_iota(I32, (16, 2048), 0) == (slot_ref[0] >> 7)
        position = lax.broadcasted_iota(I32, (16, 2048), 1)
        coded = jnp.concatenate(
            [
                jnp.where(slot_hot, (position >> 7).astype(F32), 0.0),
                jnp.where(slot_hot, (position & 127).astype(F32), 0.0),
            ],
            axis=0,
        ).astype(BF16)
        counted = dot(coded, lane_hot[...], NT)
        inverse_ref[...] = (counted[:16] * 128.0 + counted[16:]).astype(I32)

    def apply(product, carry):
        @pl.when(product == 0)
        def _():
            set_up_more()
            set_up()

        def near_part(outside):
            for n in range(16):
                a, b = n // 4, n % 4
                places = [
                    m
                    for m in range(9)
                    if outside
                    != (0 <= a + m // 3 - 1 < 4 and 0 <= b + m % 3 - 1 < 4)
                ]
                if not places:
                    continue
                sources = jnp.concatenate(
                    [
                        halo[product, a + 1 + m // 3, b + 1 + m % 3].astype(F32)[:8]
                        for m in places
                    ],
                    axis=1,
                ).astype(BF16)
                blocks = jnp.concatenate([near[a, b, m] for m in places], axis=1)
                total = dot(sources, blocks, NT)
                near_sum[n] = near_sum[n] + total if outside else total

        near_part(False)

        for copy in block_copies(product):
            copy.wait_recv()
        sums = []
        for b in range(4):
            tiles = [window[product, 1, c // 2, 2 + 2 * b + c % 2] for c in range(4)]
            sums.append((tiles[0] + tiles[1]) + (tiles[2] + tiles[3]))
        rows = [
            jnp.where(low, sums[2 * h], pltpu.roll(sums[2 * h + 1], 64, 1)) for h in range(2)
        ]
        fours[product, pair_row, patch] = dot(
            jnp.concatenate(rows, axis=1).astype(BF16), e3_twice[...], NN
        )
        for copy in top_copies(product):
            copy.start()
        for h in range(2):
            threes[product, pair_row, 0, h] = rows[h]
        step = 1 - 2 * half
        three_copies = []
        for a in range(1, 4):
            three_copies.append((threes.at[product, pair_row, 0], threes.at[product, pair_row, 0], a, 0))
        for a in range(4):
            three_copies.append(
                (
                    threes.at[product, pair_row, 0, 1 - half],
                    threes.at[product, pair_row, 1, 1 - half],
                    a,
                    step,
                )
            )
        three_copies = [
            remote(
                source,
                target,
                three_send.at[product, n],
                three_recv.at[product, n],
                top_peer(a, b),
            )
            for n, (source, target, a, b) in enumerate(three_copies)
        ]
        for copy in three_copies:
            copy.start()
        inner_cols = pl.ds(2 + 2 * half, 6)
        side_from, side_to = pl.ds(8 - 6 * half, 2), pl.ds(10 * half, 2)
        side_copies = [
            remote(
                window.at[product, 1, :, source_cols],
                window.at[product, row, :, target_cols],
                side_send.at[product, n],
                side_recv.at[product, n],
                top_peer(a, b),
            )
            for n, (row, source_cols, target_cols, a, b) in enumerate(
                (
                    (0, inner_cols, inner_cols, 1, 0),
                    (2, inner_cols, inner_cols, 3, 0),
                    (0, side_from, side_to, 1, step),
                    (1, side_from, side_to, 0, step),
                    (2, side_from, side_to, 3, step),
                )
            )
        ]
        for copy in side_copies:
            copy.start()

        @pl.when(product == 0)
        def _():
            for copy in cross_copies():
                copy.wait_recv()
            for copy in w4_copies():
                copy.start()
            w3_copy(0).start()
            w3_copy(1).start()

        for copy in halo_copies(product):
            copy.wait_recv()
        blank = jnp.zeros((16, 128), BF16)

        def clear(cells):
            for a, b in cells:
                halo[product, a, b] = blank

        @pl.when(i == 0)
        def _():
            clear([(a, b) for a in (0, 1) for b in range(8)])

        @pl.when(i == grid_rows - 1)
        def _():
            clear([(a, b) for a in (6, 7) for b in range(8)])

        @pl.when(j == 0)
        def _():
            clear([(a, b) for a in range(8) for b in (0, 1)])

        @pl.when(j == grid_cols - 1)
        def _():
            clear([(a, b) for a in range(8) for b in (6, 7)])

        near_part(True)

        @pl.when(product == 0)
        def _():
            w3_copy(1).wait_recv()
            w3_forward().start()

        def coeffs(a, b):
            return halo[product, a, b].astype(F32)[8:]

        for b in range(8):
            column = [coeffs(a, b) for a in range(8)]
            for a in range(5):
                pair_tiles[a, b] = jnp.where(low, column[a], pltpu.roll(column[a + 3], 64, 1))

        def far_parent(p, inner):
            pa, pb = p // 2, p % 2
            pairs = [pair_tiles[2 * pa + u // 6, 2 * pb + u % 6] for u in range(18)]
            far_zero[p] = far_children(
                pairs,
                lambda child, u: m0_pairs[
                    4 * (2 * pa + child // 2) + 2 * pb + child % 2, u
                ],
            )
            return inner

        lax.fori_loop(0, 4, far_parent, 0)
        place = (0, 1, 2, 3, 6, 7)
        one_pairs = [
            jnp.where(
                low,
                pltpu.roll(coeffs(place[u // 6], place[u % 6]), 64, 1),
                coeffs(place[u // 6 + 3], place[u % 6]),
            )
            for u in range(18)
        ]
        local_one = far_children(one_pairs, lambda child, u: m1_pairs[child, u])
        partly = [None] * 16
        for p in range(4):
            pa, pb = p // 2, p % 2
            transfer = e0[2 * pa : 2 * pa + 2, 2 * pb : 2 * pb + 2].reshape(256, 64)
            local_zero = far_zero[p] + dot(
                local_one[:, 64 * p : 64 * p + 64].astype(BF16), transfer, NT
            )
            for c in range(4):
                a, b = 2 * pa + c // 2, 2 * pb + c % 2
                partly[4 * a + b] = near_sum[4 * a + b] + dot(
                    local_zero[:, 64 * c : 64 * c + 64].astype(BF16), basis[a, b], NN
                )
        risen = None
        for n in range(16):
            near_sum[n] = partly[n]
            term = dot(partly[n].astype(BF16), rise[n], NN)
            risen = term if risen is None else risen + term

        for copy in side_copies:
            copy.wait_recv()
        two_sources = []
        for u in range(18):
            first = window[product, u // 6, (u // 3) % 2, 2 * own_pair + 2 * (u % 3)]
            second = window[product, u // 6, (u // 3) % 2, 2 * own_pair + 2 * (u % 3) + 1]
            two_sources.append(jnp.where(low, pltpu.roll(first, 64, 1), second))
        two_sources = jnp.where(mask2[...] > 0.0, jnp.concatenate(two_sources, axis=1), 0.0)
        far_two = dot(two_sources.astype(BF16), w2[...], NT)

        @pl.when(product == 0)
        def _():
            w3_copy(0).wait_recv()
            w3_forward().wait_recv()

        for copy in three_copies:
            copy.wait_recv()
        three_parts = ((1 - half, 1 - half), (0, half), (half, 1 - half))
        three_sources = jnp.concatenate(
            [
                threes[product, (2 * (i // 4) + 2 + u // 3) % 4, side, part_half]
                for u in range(18)
                for side, part_half in (three_parts[u % 3],)
            ],
            axis=1,
        )
        three_sources = jnp.where(mask3[...] > 0.0, three_sources, 0.0)
        far_three = dot(three_sources.astype(BF16), w3[...].reshape(64, 2304), NT)
        far_both = jnp.concatenate([far_three, far_two], axis=1)

        @pl.when(product == 0)
        def _():
            for copy in w4_copies():
                copy.wait_recv()
            rows_four = w4[...].reshape(256, 256)
            for q in range(4):
                top_matrix[0:64, 256 * q : 256 * q + 256] = dot(
                    e3_spread[q], rows_four, NN
                ).astype(BF16)
                top_matrix[64:128, 256 * q : 256 * q + 256] = jnp.zeros((64, 256), BF16)

        for copy in block_copies(product) + halo_copies(product) + three_copies + side_copies:
            copy.wait_send()
        for copy in top_copies(product):
            copy.wait_recv()
        four_sources = jnp.concatenate(
            [
                fours[product, 2 * (t // 4), t % 4] + fours[product, 2 * (t // 4) + 1, t % 4]
                for t in range(8)
            ],
            axis=1,
        )
        four_sources = jnp.where(mask4[...] > 0.0, four_sources, 0.0)
        falling = (far_both + dot(four_sources.astype(BF16), top_matrix[...], NT)).astype(BF16)

        @pl.when(product == 0)
        def _():
            window[1, 1, core, 2 + depth] = risen + dot(
                falling, turn[...], NN
            )
            for copy in block_copies(1):
                copy.start()

        fallen = dot(falling, fall[...], NN)
        results = [near_sum[n] + fallen[:, 128 * n : 128 * n + 128] for n in range(16)]
        for n in range(16):
            out_ref[product, n] = results[n]

        @pl.when(product == 0)
        def _():
            coefficients(1, results)
            for copy in halo_copies(1):
                copy.start()

        return carry

    lax.fori_loop(0, 2, apply, 0)
    for product in range(2):
        for copy in top_copies(product):
            copy.wait_send()
    for copy in [w3_copy(0), w3_copy(1), w3_forward()] + cross_copies() + w4_copies():
        copy.wait_send()


def local(
    grid_rows,
    grid_cols,
    values,
    point_slot,
    leaf_basis,
    near_blocks,
    transfer_leaf,
    transfer_mid,
    transfer_dev,
    transfer_coarse,
    coupling_leaf,
    coupling_mid,
    coupling_dev,
    coupling_coarse,
    coupling_top,
):
    whole = pl.BlockSpec(memory_space=pltpu.VMEM)
    left = pl.BlockSpec(memory_space=pl.ANY)
    dma = pltpu.SemaphoreType.DMA
    params = pltpu.CompilerParams(vmem_limit_bytes=VMEM_LIMIT)
    products, inverse = pl.pallas_call(
        functools.partial(main_kernel, grid_rows, grid_cols),
        out_shape=(
            jax.ShapeDtypeStruct((2, 16, 8, 128), F32),
            jax.ShapeDtypeStruct((16, 128), I32),
        ),
        in_specs=[whole] * 3 + [left] * LOCAL_ARRAYS,
        out_specs=(whole,) * 2,
        scratch_shapes=[
            pltpu.VMEM((4, 4, 64, 128), BF16),
            pltpu.VMEM((4, 4, 9, 128, 128), BF16),
            pltpu.VMEM((4, 4, 64, 64), BF16),
            pltpu.VMEM((2, 2, 64, 64), BF16),
            pltpu.VMEM((1, 1, 64, 64), BF16),
            pltpu.VMEM((1, 4, 64, 64), BF16),
            pltpu.VMEM((4, 4, 36, 64, 64), BF16),
            pltpu.VMEM((2, 2, 36, 64, 64), BF16),
            pltpu.VMEM((1, 1, 36, 64, 64), BF16),
            pltpu.VMEM((1, 1, 36, 16, 64), BF16),
            pltpu.VMEM((16, 18, 64, 128), BF16),
            pltpu.VMEM((4, 18, 64, 128), BF16),
            pltpu.VMEM((64, 2304), BF16),
            pltpu.VMEM((4, 16, 2304), BF16),
            pltpu.VMEM((16, 16, 256), BF16),
            pltpu.VMEM((16, 256), F32),
            pltpu.VMEM((16, 256), BF16),
            pltpu.VMEM((256, 128), BF16),
            pltpu.VMEM((4, 64, 256), BF16),
            pltpu.VMEM((128, 1024), BF16),
            pltpu.VMEM((16, 128, 128), BF16),
            pltpu.VMEM((128, 2048), BF16),
            pltpu.VMEM((128, 128), BF16),
            pltpu.VMEM((128, 2048), BF16),
            pltpu.VMEM((8, 2304), F32),
            pltpu.VMEM((8, 2304), F32),
            pltpu.VMEM((8, 1024), F32),
            pltpu.VMEM((2, 8, 8, 16, 128), BF16),
            pltpu.VMEM((2, 3, 2, 12, 8, 128), F32),
            pltpu.VMEM((2, 4, 2, 2, 8, 128), F32),
            pltpu.VMEM((2, 4, 4, 8, 128), F32),
            pltpu.VMEM((5, 8, 8, 128), F32),
            pltpu.VMEM((16, 8, 128), F32),
            pltpu.VMEM((4, 8, 256), F32),
            dma((LOCAL_ARRAYS,)),
            dma((2, 15)),
            dma((2, 15)),
            dma((2, 15)),
            dma((2, 15)),
            dma((2, 7)),
            dma((2, 7)),
            dma((2, 5)),
            dma((2, 5)),
            dma((2, 8)),
            dma((2, 8)),
            dma((3,)),
            dma((3,)),
            dma((2,)),
            dma((2,)),
            dma((14,)),
            dma((14,)),
        ],
        compiler_params=pltpu.CompilerParams(
            collective_id=0, has_side_effects=True, vmem_limit_bytes=VMEM_LIMIT
        ),
    )(
        jnp.transpose(values, (1, 2, 0, 3)),
        point_slot,
        coupling_top,
        jnp.swapaxes(leaf_basis, 2, 3),
        near_blocks,
        transfer_leaf,
        transfer_mid,
        transfer_dev,
        transfer_coarse,
        coupling_leaf,
        coupling_mid,
        coupling_dev,
        coupling_coarse,
    )
    placed = jax.ShapeDtypeStruct(values.shape, F32)
    return pl.pallas_call(
        place_kernel,
        out_shape=(placed, placed),
        in_specs=[whole] * 2,
        out_specs=(whole,) * 2,
        compiler_params=params,
    )(products, inverse)


def solution(mesh):
    placed = (
        P(None, "gx", "gy", None),
        P("gx", "gy", None),
        P("gx", "gy", None, None),
        P("gx", "gy", None, None, None),
        P("gx", "gy", None, None),
        P("gx", "gy", None, None),
        P("gx", "gy", None, None),
        P(),
        P("gx", "gy", None, None, None),
        P("gx", "gy", None, None, None),
        P("gx", "gy", None, None, None),
        P("gx", "gy", None, None, None),
        P("gx", "gy", None, None, None),
    )
    return jax.shard_map(
        functools.partial(local, mesh.shape["gx"], mesh.shape["gy"]),
        mesh=mesh,
        in_specs=placed,
        out_specs=(P(None, "gx", "gy", None), P(None, "gx", "gy", None)),
        check_vma=False,
    )
```

```python
import functools

import jax
import jax.numpy as jnp
from jax import lax
from jax.experimental import pallas as pl
from jax.experimental.pallas import tpu as pltpu
from jax.sharding import PartitionSpec as P

F32 = jnp.float32
BF16 = jnp.bfloat16
I32 = jnp.int32
MESH = pl.DeviceIdType.MESH
NN = (((1,), (0,)), ((), ()))
NT = (((1,), (1,)), ((), ()))
VMEM_LIMIT = 56 * 2**20

BLOCK_PEERS = [(a, b) for b in (4, 3, 5, 2, 6, 1, 7) for a in (1, 0)] + [(1, 0)]
TOP_PEERS = [(2, 2), (2, 1), (2, 3), (1, 2), (3, 2), (1, 1), (1, 3), (3, 1), (3, 3)] + [
    (2, 0),
    (0, 2),
    (1, 0),
    (3, 0),
    (0, 1),
    (0, 3),
]
HALF_PEERS = [(a, b) for a in range(2) for b in range(4) if a or b]
BESIDE = [(a, b) for a in (-1, 0, 1) for b in (-1, 0, 1) if a or b]
LOCAL_ARRAYS = 10


def dot(left, right, dims):
    return lax.dot_general(left, right, dims, preferred_element_type=F32)


def permute(blocks, index_row):
    index = jnp.broadcast_to(index_row, (8, 128))
    lane = index & 127
    source = index >> 7
    result = None
    for block, piece in enumerate(blocks):
        taken = jnp.take_along_axis(piece, lane, axis=1, mode="promise_in_bounds")
        result = taken if result is None else jnp.where(source == block, taken, result)
    return result


def place_kernel(ordered_ref, inverse_ref, first_ref, second_ref):
    for which, placed_ref in enumerate((first_ref, second_ref)):
        pieces = [ordered_ref[which, s] for s in range(16)]
        for m in range(16):
            result = permute(pieces, inverse_ref[m : m + 1])
            for r in range(8):
                placed_ref[r, 0, 0:1, 128 * m : 128 * m + 128] = result[r : r + 1]


def keeps(slot, child):
    return abs(slot // 6 - 2 - child // 2) > 1 or abs(slot % 6 - 2 - child % 2) > 1


def far_children(pairs, weight):
    low = lax.broadcasted_iota(I32, (8, 128), 1) < 64
    zero = jnp.zeros((8, 128), F32)
    sources, matrices = [], []
    for u, pair in pairs:
        rows = []
        for child in range(4):
            first, second = keeps(2 * u, child), keeps(2 * u + 1, child)
            if first and second:
                rows.append(pair)
            elif first:
                rows.append(jnp.where(low, pair, zero))
            elif second:
                rows.append(jnp.where(low, zero, pair))
            else:
                rows.append(zero)
        sources.append(jnp.concatenate(rows, axis=0).astype(BF16))
        matrices.append(jnp.concatenate([weight(child, u) for child in range(4)], axis=0))
    total = dot(jnp.concatenate(sources, axis=1), jnp.concatenate(matrices, axis=1), NT)
    owner = lax.broadcasted_iota(I32, (8, 256), 1) >> 6
    result = jnp.zeros((8, 256), F32)
    for child in range(4):
        result = result + jnp.where(owner == child, total[8 * child : 8 * child + 8], 0.0)
    return result


def window_mask(row, col, rows, cols, by_box):
    slot = lax.broadcasted_iota(I32, (8, 2304), 1) >> 6
    if by_box:
        box = slot >> 2
        box_row = (box * 11) >> 5
        slot_row = 2 * box_row + (slot & 1)
        slot_col = 2 * (box - 3 * box_row) + ((slot >> 1) & 1)
    else:
        slot_row = (slot * 43) >> 8
        slot_col = slot - 6 * slot_row
    source_row = slot_row + 2 * (row // 2) - 2
    source_col = slot_col + 2 * (col // 2) - 2
    inside = (source_row >= 0) & (source_row < rows) & (source_col >= 0) & (source_col < cols)
    apart = (jnp.abs(source_row - row) > 1) | (jnp.abs(source_col - col) > 1)
    return jnp.where(inside & apart, 1.0, 0.0)


def strip(step):
    return {-1: (2, 6, 2), 0: (2, 2, 4), 1: (4, 0, 2)}[step]


def main_kernel(
    grid_rows,
    grid_cols,
    values_ref,
    slot_ref,
    top_ref,
    basis_any,
    near_any,
    e0_any,
    e1_any,
    e2_any,
    e3_any,
    m0_any,
    m1_any,
    m2_any,
    m3_any,
    out_ref,
    inverse_ref,
    basis,
    near,
    e0,
    e1,
    e2,
    e3,
    m0,
    m1,
    m2,
    m3,
    m0_pairs,
    m1_pairs,
    w2,
    w3,
    w4,
    part_wide,
    part,
    e3_twice,
    e3_spread,
    top_matrix,
    rise,
    fall,
    turn,
    lane_hot,
    mask2,
    mask3,
    mask4,
    halo,
    window,
    twos,
    threes,
    fours,
    pair_tiles,
    near_sum,
    far_zero,
    local_sem,
    block_send,
    block_recv,
    top_send,
    top_recv,
    three_send,
    three_recv,
    side_send,
    side_recv,
    halo_send,
    halo_recv,
    w3_send,
    w3_recv,
    cross_send,
    cross_recv,
    w4_send,
    w4_recv,
):
    i = lax.axis_index("gx")
    j = lax.axis_index("gy")
    pair_row, core = i // 2, i % 2
    patch, depth = j // 8, j % 8
    half = depth // 4
    own_pair = depth // 2

    def block_peer(a, b):
        return (2 * pair_row + (core + a) % 2, 8 * patch + (depth + b) % 8)

    def half_peer(a, b):
        return (2 * pair_row + (core + a) % 2, 8 * patch + 4 * half + (depth + b) % 4)

    def top_peer(a, b):
        return ((i + 2 * a) % grid_rows, (j + 8 * b + grid_cols) % grid_cols)

    def beside(a, b):
        return ((i + a + grid_rows) % grid_rows, (j + b + grid_cols) % grid_cols)

    def remote(source, target, send, recv, peer):
        return pltpu.make_async_remote_copy(
            src_ref=source,
            dst_ref=target,
            send_sem=send,
            recv_sem=recv,
            device_id=peer,
            device_id_type=MESH,
        )

    barrier = pltpu.get_barrier_semaphore()
    for a, b in TOP_PEERS:
        pl.semaphore_signal(barrier, 1, device_id=top_peer(a, b), device_id_type=MESH)
    for a, b in BLOCK_PEERS:
        pl.semaphore_signal(barrier, 1, device_id=block_peer(a, b), device_id_type=MESH)
    for a, b in BESIDE:
        pl.semaphore_signal(barrier, 1, device_id=beside(a, b), device_id_type=MESH)

    e3_own = e3_any.at[pl.ds(pair_row, 1), pl.ds(4 * patch, 4)]
    staged = [
        (basis_any, basis),
        (e0_any, e0),
        (e1_any, e1),
        (e2_any, e2),
        (m3_any, m3),
        (m2_any, m2),
        (e3_own, e3),
        (m1_any, m1),
        (m0_any, m0),
        (near_any, near),
    ]
    loads = [
        pltpu.make_async_copy(source, target, local_sem.at[n])
        for n, (source, target) in enumerate(staged)
    ]
    for load in loads:
        load.start()

    low = lax.broadcasted_iota(I32, (8, 128), 1) < 64

    def coefficients(product, leaf):
        level_zero = [dot(leaf[n].astype(BF16), basis[n // 4, n % 4], NT) for n in range(16)]
        level_one = []
        for p in range(4):
            pa, pb = p // 2, p % 2
            children = jnp.concatenate(
                [level_zero[4 * (2 * pa + c // 2) + 2 * pb + c % 2] for c in range(4)], axis=1
            ).astype(BF16)
            transfer = e0[2 * pa : 2 * pa + 2, 2 * pb : 2 * pb + 2].reshape(256, 64)
            level_one.append(dot(children, transfer, NN))
        for n in range(16):
            a, b = n // 4, n % 4
            coeffs = jnp.concatenate(
                [level_zero[n], level_one[2 * (a % 2) + b % 2]], axis=1
            )
            halo[product, 2 + a, 2 + b] = jnp.concatenate([leaf[n], coeffs], axis=0).astype(BF16)
        return level_one

    slots = slot_ref[0]
    slot_lane = lax.broadcasted_iota(I32, (128, 2048), 0) == (slots & 127)
    lane_hot[...] = jnp.where(slot_lane, 1.0, 0.0).astype(BF16)
    values = values_ref[0, 0].astype(F32)
    stacked = jnp.concatenate([values[:, 128 * s : 128 * s + 128] for s in range(16)], axis=0)
    candidates = dot(stacked.astype(BF16), lane_hot[...], NN)
    slot_block = jnp.broadcast_to(slots >> 7, (8, 2048))
    ordered = jnp.zeros((8, 2048), F32)
    for s in range(16):
        ordered = jnp.where(slot_block == s, candidates[8 * s : 8 * s + 8], ordered)

    for n in range(4):
        loads[n].wait()
    level_one = coefficients(0, [ordered[:, 128 * n : 128 * n + 128] for n in range(16)])
    level_two = dot(
        jnp.concatenate(level_one, axis=1).astype(BF16), e1[...].reshape(256, 64), NN
    )
    term = dot(level_two.astype(BF16), e2[0, 0], NN)
    window[0, core, depth] = jnp.concatenate(
        [term, level_two], axis=1
    )

    def block_copies(product):
        copies = []
        for n, (a, b) in enumerate(BLOCK_PEERS):
            copies.append(
                remote(
                    window.at[product, core, depth],
                    window.at[product, core, depth],
                    block_send.at[product, n],
                    block_recv.at[product, n],
                    block_peer(a, b),
                )
            )
        return copies

    def halo_copies(product):
        copies = []
        for n, (a, b) in enumerate(BESIDE):
            row_from, row_to, row_count = strip(a)
            col_from, col_to, col_count = strip(b)
            copies.append(
                remote(
                    halo.at[product, pl.ds(row_from, row_count), pl.ds(col_from, col_count)],
                    halo.at[product, pl.ds(row_to, row_count), pl.ds(col_to, col_count)],
                    halo_send.at[product, n],
                    halo_recv.at[product, n],
                    beside(a, b),
                )
            )
        return copies

    own_three = 2 * (i % 2) + j % 2
    own_four = 8 * (pair_row % 2) + 4 * (own_pair % 2) + own_three
    other_four = 8 - 8 * (pair_row % 2) + 4 * (own_pair % 2) + own_three
    next_three = 2 * (i % 2) + 1 - j % 2
    three_peers = [
        (2 * (i // 2) + (i + a) % 2, 2 * (j // 2) + (j + b) % 2) for a, b in ((1, 0), (0, 1))
    ]

    def w3_copy(n):
        return remote(
            w3.at[own_three], w3.at[own_three], w3_send.at[n], w3_recv.at[n], three_peers[n]
        )

    def w3_forward():
        return remote(
            w3.at[next_three], w3.at[next_three], w3_send.at[2], w3_recv.at[2], three_peers[0]
        )

    def cross_copies():
        return [
            remote(
                part, w4.at[own_four], cross_send.at[n], cross_recv.at[n], top_peer(a, 0)
            )
            for n, a in enumerate((2, 3 - 2 * (pair_row % 2)))
        ]

    def w4_copies():
        return [
            remote(
                w4.at[which],
                w4.at[which],
                w4_send.at[7 * m + n],
                w4_recv.at[7 * m + n],
                half_peer(a, b),
            )
            for m, which in enumerate((own_four, other_four))
            for n, (a, b) in enumerate(HALF_PEERS)
        ]

    def top_copies(product):
        return [
            remote(
                fours.at[product, pair_row, patch],
                fours.at[product, pair_row, patch],
                top_send.at[product, n],
                top_recv.at[product, n],
                top_peer(a, b),
            )
            for n, (a, b) in enumerate(TOP_PEERS)
        ]

    for t in range(16):
        part_wide[4 * (t // 4) : 4 * (t // 4) + 4, 64 * (t % 4) : 64 * (t % 4) + 64] = top_ref[
            0, 0, t
        ].astype(F32)
    part[...] = part_wide[...].astype(BF16)
    loads[4].wait()
    for u in range(18):
        w3[own_three, :, 128 * u : 128 * u + 128] = jnp.concatenate(
            [m3[0, 0, 2 * u], m3[0, 0, 2 * u + 1]], axis=1
        )
    loads[6].wait()
    coarse = e3[...].reshape(256, 64)
    first_half = lax.broadcasted_iota(I32, (256, 64), 0) < 128
    nothing = jnp.zeros((256, 64), F32)
    coarse = coarse.astype(F32)
    e3_twice[...] = jnp.concatenate(
        [jnp.where(first_half, coarse, nothing), jnp.where(first_half, nothing, coarse)], axis=1
    ).astype(BF16)
    loads[5].wait()

    pl.semaphore_wait(barrier, len(TOP_PEERS) + len(BLOCK_PEERS) + len(BESIDE))
    for copy in block_copies(0):
        copy.start()
    for copy in halo_copies(0):
        copy.start()
    for copy in cross_copies():
        copy.start()
    w3_copy(0).start()
    w3_copy(1).start()

    def set_up():
        loads[7].wait()
        for n in range(4):
            for u in range(18):
                m1_pairs[n, u] = jnp.concatenate(
                    [m1[n // 2, n % 2, 2 * u], m1[n // 2, n % 2, 2 * u + 1]], axis=1
                )
        loads[8].wait()

        def pack(n, inner):
            for u in range(18):
                m0_pairs[n, u] = jnp.concatenate(
                    [m0[n // 4, n % 4, 2 * u], m0[n // 4, n % 4, 2 * u + 1]], axis=1
                )
            return inner

        lax.fori_loop(0, 16, pack, 0)

    def set_up_more():
        for u in range(18):
            first = 12 * (u // 6) + u % 6
            w2[:, 128 * u : 128 * u + 128] = jnp.concatenate(
                [m2[0, 0, first], m2[0, 0, first + 6]], axis=1
            )
        mask2[...] = window_mask(i, j, grid_rows, grid_cols, True)
        mask3[...] = window_mask(i // 2, j // 2, grid_rows // 2, grid_cols // 2, False)
        top_box = lax.broadcasted_iota(I32, (8, 1024), 1) >> 6
        apart = (jnp.abs((top_box >> 3) - i // 4) > 1) | (jnp.abs((top_box & 7) - j // 4) > 1)
        mask4[...] = jnp.where(apart, 1.0, 0.0)
        spread_row = lax.broadcasted_iota(I32, (64, 256), 0)
        spread_col = lax.broadcasted_iota(I32, (64, 256), 1)
        chosen = spread_row == (spread_col >> 4) * 4 + (spread_col & 3)
        spread = dot(e3[0, own_pair], jnp.where(chosen, 1.0, 0.0).astype(BF16), NN)
        for q in range(4):
            e3_spread[q] = jnp.where(((spread_col >> 2) & 3) == q, spread, 0.0).astype(BF16)
        total = None
        for n in range(16):
            a, b = n // 4, n % 4
            two = dot(e0[a, b], e1[a // 2, b // 2], NN)
            both = jnp.concatenate([dot(two.astype(BF16), e2[0, 0], NN), two], axis=1)
            up = dot(basis[a, b].astype(F32).T.astype(BF16), both.astype(BF16), NN)
            rise[n] = up.astype(BF16)
            fall[:, 128 * n : 128 * n + 128] = up.T.astype(BF16)
            around = dot(up.T.astype(BF16), up.astype(BF16), NN)
            total = around if total is None else total + around
        turn[...] = total.astype(BF16)
        slot_hot = lax.broadcasted_iota(I32, (16, 2048), 0) == (slot_ref[0] >> 7)
        position = lax.broadcasted_iota(I32, (16, 2048), 1)
        coded = jnp.concatenate(
            [
                jnp.where(slot_hot, (position >> 7).astype(F32), 0.0),
                jnp.where(slot_hot, (position & 127).astype(F32), 0.0),
            ],
            axis=0,
        ).astype(BF16)
        counted = dot(coded, lane_hot[...], NT)
        inverse_ref[...] = (counted[:16] * 128.0 + counted[16:]).astype(I32)

    def near_part(product, outside):
        for n in range(16):
            a, b = n // 4, n % 4
            places = [
                m
                for m in range(9)
                if outside
                != (0 <= a + m // 3 - 1 < 4 and 0 <= b + m % 3 - 1 < 4)
            ]
            if not places:
                continue
            sources = jnp.concatenate(
                [
                    halo[product, a + 1 + m // 3, b + 1 + m % 3].astype(F32)[:8]
                    for m in places
                ],
                axis=1,
            ).astype(BF16)
            blocks = jnp.concatenate([near[a, b, m] for m in places], axis=1)
            total = dot(sources, blocks, NT)
            near_sum[n] = near_sum[n] + total if outside else total

    def coeffs(product, a, b):
        return halo[product, a, b].astype(F32)[8:]

    def pair_part(product, outside):
        for a in range(8):
            for b in range(4):
                if outside != (2 <= a < 6 and 1 <= b < 3):
                    pair_tiles[a, b] = jnp.where(
                        low,
                        coeffs(product, a, 2 * b),
                        pltpu.roll(coeffs(product, a, 2 * b + 1), 64, 1),
                    )
        for p in range(4):
            pa, pb = p // 2, p % 2
            pairs = []
            for u in range(18):
                a, b = 2 * pa + u // 3, pb + u % 3
                if outside != (2 <= a < 6 and 1 <= b < 3):
                    pairs.append((u, pair_tiles[a, b]))
            total = far_children(
                pairs,
                lambda child, u: m0_pairs[4 * (2 * pa + child // 2) + 2 * pb + child % 2, u],
            )
            far_zero[p] = far_zero[p] + total if outside else total

    def interior(product):
        near_part(product, False)
        pair_part(product, False)

    def apply(product, carry):
        @pl.when(product == 0)
        def _():
            set_up_more()
            set_up()

        for copy in block_copies(product):
            copy.wait_recv()
        sums = []
        for b in range(4):
            tiles = [window[product, c // 2, 2 * b + c % 2] for c in range(4)]
            sums.append((tiles[0] + tiles[1]) + (tiles[2] + tiles[3]))
        rows = [
            jnp.where(low, sums[2 * h], pltpu.roll(sums[2 * h + 1], 64, 1)) for h in range(2)
        ]
        fours[product, pair_row, patch] = dot(
            jnp.concatenate(rows, axis=1).astype(BF16), e3_twice[...], NN
        )
        for copy in top_copies(product):
            copy.start()
        for h in range(2):
            threes[product, pair_row, 0, h] = rows[h]
        step = 1 - 2 * half
        three_copies = []
        for a in range(1, 4):
            three_copies.append((threes.at[product, pair_row, 0], threes.at[product, pair_row, 0], a, 0))
        for a in range(4):
            three_copies.append(
                (
                    threes.at[product, pair_row, 0, 1 - half],
                    threes.at[product, pair_row, 1, 1 - half],
                    a,
                    step,
                )
            )
        three_copies = [
            remote(
                source,
                target,
                three_send.at[product, n],
                three_recv.at[product, n],
                top_peer(a, b),
            )
            for n, (source, target, a, b) in enumerate(three_copies)
        ]
        for copy in three_copies:
            copy.start()
        @pl.when(product == 0)
        def _():
            for copy in cross_copies():
                copy.wait_recv()
            for copy in w4_copies():
                copy.start()

        for b in range(4):
            pieces = [
                jnp.where(
                    low,
                    pltpu.roll(window[product, 0, 2 * b + c], 64, 1),
                    window[product, 1, 2 * b + c],
                )
                for c in range(2)
            ]
            twos[product, 1, 1 + b] = jnp.concatenate(pieces, axis=0).astype(BF16)
        inner = pl.ds(1, 4)
        side_from, side_to = pl.ds(4 - 3 * half, 1), pl.ds(5 * half, 1)
        side_copies = [
            remote(
                twos.at[product, 1, source],
                twos.at[product, row, target],
                side_send.at[product, n],
                side_recv.at[product, n],
                top_peer(a, b),
            )
            for n, (row, source, target, a, b) in enumerate(
                (
                    (0, inner, inner, 1, 0),
                    (2, inner, inner, 3, 0),
                    (0, side_from, side_to, 1, step),
                    (1, side_from, side_to, 0, step),
                    (2, side_from, side_to, 3, step),
                )
            )
        ]
        for copy in side_copies:
            copy.start()

        @pl.when(product == 0)
        def _():
            loads[9].wait()
            interior(0)

        for copy in halo_copies(product):
            copy.wait_recv()
        blank = jnp.zeros((16, 128), BF16)

        def clear(cells):
            for a, b in cells:
                halo[product, a, b] = blank

        @pl.when(i == 0)
        def _():
            clear([(a, b) for a in (0, 1) for b in range(8)])

        @pl.when(i == grid_rows - 1)
        def _():
            clear([(a, b) for a in (6, 7) for b in range(8)])

        @pl.when(j == 0)
        def _():
            clear([(a, b) for a in range(8) for b in (0, 1)])

        @pl.when(j == grid_cols - 1)
        def _():
            clear([(a, b) for a in range(8) for b in (6, 7)])

        near_part(product, True)

        @pl.when(product == 0)
        def _():
            w3_copy(1).wait_recv()
            w3_forward().start()

        pair_part(product, True)
        one_pairs = []
        for u in range(18):
            a, b = (0, 1, 2, 3, 6, 7)[u // 3], (0, 2, 6)[u % 3]
            one_pairs.append(
                (
                    u,
                    jnp.where(
                        low,
                        pltpu.roll(coeffs(product, a, b), 64, 1),
                        coeffs(product, a, b + 1),
                    ),
                )
            )
        local_one = far_children(one_pairs, lambda child, u: m1_pairs[child, u])
        partly = [None] * 16
        for p in range(4):
            pa, pb = p // 2, p % 2
            transfer = e0[2 * pa : 2 * pa + 2, 2 * pb : 2 * pb + 2].reshape(256, 64)
            local_zero = far_zero[p] + dot(
                local_one[:, 64 * p : 64 * p + 64].astype(BF16), transfer, NT
            )
            for c in range(4):
                a, b = 2 * pa + c // 2, 2 * pb + c % 2
                partly[4 * a + b] = near_sum[4 * a + b] + dot(
                    local_zero[:, 64 * c : 64 * c + 64].astype(BF16), basis[a, b], NN
                )
        risen = None
        for n in range(16):
            near_sum[n] = partly[n]
            term = dot(partly[n].astype(BF16), rise[n], NN)
            risen = term if risen is None else risen + term

        for copy in side_copies:
            copy.wait_recv()
        two_sources = []
        for u in range(18):
            if u % 2 == 0:
                tile = twos[product, u // 6, own_pair + (u // 2) % 3].astype(F32)
            two_sources.append(tile[8 * (u % 2) :][:8])
        two_sources = jnp.where(mask2[...] > 0.0, jnp.concatenate(two_sources, axis=1), 0.0)
        far_two = dot(two_sources.astype(BF16), w2[...], NT)

        @pl.when(product == 0)
        def _():
            w3_copy(0).wait_recv()
            w3_forward().wait_recv()

        for copy in three_copies:
            copy.wait_recv()
        three_parts = ((1 - half, 1 - half), (0, half), (half, 1 - half))
        three_sources = jnp.concatenate(
            [
                threes[product, (2 * (i // 4) + 2 + u // 3) % 4, side, part_half]
                for u in range(18)
                for side, part_half in (three_parts[u % 3],)
            ],
            axis=1,
        )
        three_sources = jnp.where(mask3[...] > 0.0, three_sources, 0.0)
        far_three = dot(three_sources.astype(BF16), w3[...].reshape(64, 2304), NT)
        far_both = jnp.concatenate([far_three, far_two], axis=1)

        @pl.when(product == 0)
        def _():
            for copy in w4_copies():
                copy.wait_recv()
            rows_four = w4[...].reshape(256, 256)
            for q in range(4):
                top_matrix[0:64, 256 * q : 256 * q + 256] = dot(
                    e3_spread[q], rows_four, NN
                ).astype(BF16)
                top_matrix[64:128, 256 * q : 256 * q + 256] = jnp.zeros((64, 256), BF16)

        for copy in block_copies(product) + halo_copies(product) + three_copies + side_copies:
            copy.wait_send()
        for copy in top_copies(product):
            copy.wait_recv()
        four_sources = jnp.concatenate(
            [
                fours[product, 2 * (t // 4), t % 4] + fours[product, 2 * (t // 4) + 1, t % 4]
                for t in range(8)
            ],
            axis=1,
        )
        four_sources = jnp.where(mask4[...] > 0.0, four_sources, 0.0)
        falling = (far_both + dot(four_sources.astype(BF16), top_matrix[...], NT)).astype(BF16)

        @pl.when(product == 0)
        def _():
            window[1, core, depth] = risen + dot(
                falling, turn[...], NN
            )
            for copy in block_copies(1):
                copy.start()

        fallen = dot(falling, fall[...], NN)
        results = [near_sum[n] + fallen[:, 128 * n : 128 * n + 128] for n in range(16)]
        for n in range(16):
            out_ref[product, n] = results[n]

        @pl.when(product == 0)
        def _():
            coefficients(1, results)
            for copy in halo_copies(1):
                copy.start()
            interior(1)

        return carry

    lax.fori_loop(0, 2, apply, 0)
    for product in range(2):
        for copy in top_copies(product):
            copy.wait_send()
    for copy in [w3_copy(0), w3_copy(1), w3_forward()] + cross_copies() + w4_copies():
        copy.wait_send()


def local(
    grid_rows,
    grid_cols,
    values,
    point_slot,
    leaf_basis,
    near_blocks,
    transfer_leaf,
    transfer_mid,
    transfer_dev,
    transfer_coarse,
    coupling_leaf,
    coupling_mid,
    coupling_dev,
    coupling_coarse,
    coupling_top,
):
    whole = pl.BlockSpec(memory_space=pltpu.VMEM)
    left = pl.BlockSpec(memory_space=pl.ANY)
    dma = pltpu.SemaphoreType.DMA
    params = pltpu.CompilerParams(vmem_limit_bytes=VMEM_LIMIT)
    products, inverse = pl.pallas_call(
        functools.partial(main_kernel, grid_rows, grid_cols),
        out_shape=(
            jax.ShapeDtypeStruct((2, 16, 8, 128), F32),
            jax.ShapeDtypeStruct((16, 128), I32),
        ),
        in_specs=[whole] * 3 + [left] * LOCAL_ARRAYS,
        out_specs=(whole,) * 2,
        scratch_shapes=[
            pltpu.VMEM((4, 4, 64, 128), BF16),
            pltpu.VMEM((4, 4, 9, 128, 128), BF16),
            pltpu.VMEM((4, 4, 64, 64), BF16),
            pltpu.VMEM((2, 2, 64, 64), BF16),
            pltpu.VMEM((1, 1, 64, 64), BF16),
            pltpu.VMEM((1, 4, 64, 64), BF16),
            pltpu.VMEM((4, 4, 36, 64, 64), BF16),
            pltpu.VMEM((2, 2, 36, 64, 64), BF16),
            pltpu.VMEM((1, 1, 36, 64, 64), BF16),
            pltpu.VMEM((1, 1, 36, 16, 64), BF16),
            pltpu.VMEM((16, 18, 64, 128), BF16),
            pltpu.VMEM((4, 18, 64, 128), BF16),
            pltpu.VMEM((64, 2304), BF16),
            pltpu.VMEM((4, 16, 2304), BF16),
            pltpu.VMEM((16, 16, 256), BF16),
            pltpu.VMEM((16, 256), F32),
            pltpu.VMEM((16, 256), BF16),
            pltpu.VMEM((256, 128), BF16),
            pltpu.VMEM((4, 64, 256), BF16),
            pltpu.VMEM((128, 1024), BF16),
            pltpu.VMEM((16, 128, 128), BF16),
            pltpu.VMEM((128, 2048), BF16),
            pltpu.VMEM((128, 128), BF16),
            pltpu.VMEM((128, 2048), BF16),
            pltpu.VMEM((8, 2304), F32),
            pltpu.VMEM((8, 2304), F32),
            pltpu.VMEM((8, 1024), F32),
            pltpu.VMEM((2, 8, 8, 16, 128), BF16),
            pltpu.VMEM((2, 2, 8, 8, 128), F32),
            pltpu.VMEM((2, 3, 6, 16, 128), BF16),
            pltpu.VMEM((2, 4, 2, 2, 8, 128), F32),
            pltpu.VMEM((2, 4, 4, 8, 128), F32),
            pltpu.VMEM((8, 4, 8, 128), F32),
            pltpu.VMEM((16, 8, 128), F32),
            pltpu.VMEM((4, 8, 256), F32),
            dma((LOCAL_ARRAYS,)),
            dma((2, 15)),
            dma((2, 15)),
            dma((2, 15)),
            dma((2, 15)),
            dma((2, 7)),
            dma((2, 7)),
            dma((2, 5)),
            dma((2, 5)),
            dma((2, 8)),
            dma((2, 8)),
            dma((3,)),
            dma((3,)),
            dma((2,)),
            dma((2,)),
            dma((14,)),
            dma((14,)),
        ],
        compiler_params=pltpu.CompilerParams(
            collective_id=0, has_side_effects=True, vmem_limit_bytes=VMEM_LIMIT
        ),
    )(
        jnp.transpose(values, (1, 2, 0, 3)),
        point_slot,
        coupling_top,
        jnp.swapaxes(leaf_basis, 2, 3),
        near_blocks,
        transfer_leaf,
        transfer_mid,
        transfer_dev,
        transfer_coarse,
        coupling_leaf,
        coupling_mid,
        coupling_dev,
        coupling_coarse,
    )
    placed = jax.ShapeDtypeStruct(values.shape, F32)
    return pl.pallas_call(
        place_kernel,
        out_shape=(placed, placed),
        in_specs=[whole] * 2,
        out_specs=(whole,) * 2,
        compiler_params=params,
    )(products, inverse)


def solution(mesh):
    placed = (
        P(None, "gx", "gy", None),
        P("gx", "gy", None),
        P("gx", "gy", None, None),
        P("gx", "gy", None, None, None),
        P("gx", "gy", None, None),
        P("gx", "gy", None, None),
        P("gx", "gy", None, None),
        P(),
        P("gx", "gy", None, None, None),
        P("gx", "gy", None, None, None),
        P("gx", "gy", None, None, None),
        P("gx", "gy", None, None, None),
        P("gx", "gy", None, None, None),
    )
    return jax.shard_map(
        functools.partial(local, mesh.shape["gx"], mesh.shape["gy"]),
        mesh=mesh,
        in_specs=placed,
        out_specs=(P(None, "gx", "gy", None), P(None, "gx", "gy", None)),
        check_vma=False,
    )
```

```python
import functools

import jax
import jax.numpy as jnp
from jax import lax
from jax.experimental import pallas as pl
from jax.experimental.pallas import tpu as pltpu
from jax.sharding import PartitionSpec as P

F32 = jnp.float32
BF16 = jnp.bfloat16
I32 = jnp.int32
MESH = pl.DeviceIdType.MESH
NN = (((1,), (0,)), ((), ()))
NT = (((1,), (1,)), ((), ()))
VMEM_LIMIT = 56 * 2**20

BLOCK_PEERS = [(a, b) for b in (4, 3, 5, 2, 6, 1, 7) for a in (1, 0)] + [(1, 0)]
TOP_PEERS = [(2, 2), (2, 1), (2, 3), (1, 2), (3, 2), (1, 1), (1, 3), (3, 1), (3, 3)] + [
    (2, 0),
    (0, 2),
    (1, 0),
    (3, 0),
    (0, 1),
    (0, 3),
]
HALF_PEERS = [(a, b) for a in range(2) for b in range(4) if a or b]
BESIDE = [(a, b) for a in (-1, 0, 1) for b in (-1, 0, 1) if a or b]
LOCAL_ARRAYS = 10


def dot(left, right, dims):
    return lax.dot_general(left, right, dims, preferred_element_type=F32)


def permute(blocks, index_row):
    index = jnp.broadcast_to(index_row, (8, 128))
    lane = index & 127
    source = index >> 7
    result = None
    for block, piece in enumerate(blocks):
        taken = jnp.take_along_axis(piece, lane, axis=1, mode="promise_in_bounds")
        result = taken if result is None else jnp.where(source == block, taken, result)
    return result


def place_kernel(
    ordered_any,
    inverse_any,
    first_any,
    second_any,
    ordered,
    inverse,
    placed,
    load_sem,
    store_sem,
):
    loads = [
        pltpu.make_async_copy(inverse_any, inverse, load_sem.at[2]),
        pltpu.make_async_copy(ordered_any.at[0], ordered.at[0], load_sem.at[0]),
        pltpu.make_async_copy(ordered_any.at[1], ordered.at[1], load_sem.at[1]),
    ]
    stores = [
        pltpu.make_async_copy(placed.at[0], first_any, store_sem.at[0]),
        pltpu.make_async_copy(placed.at[1], second_any, store_sem.at[1]),
    ]
    for load in loads:
        load.start()
    loads[0].wait()
    for which in range(2):
        loads[1 + which].wait()
        pieces = [ordered[which, s] for s in range(16)]
        for m in range(16):
            result = permute(pieces, inverse[m : m + 1])
            for r in range(8):
                placed[which, r, 0, 0:1, 128 * m : 128 * m + 128] = result[r : r + 1]
        stores[which].start()
    for store in stores:
        store.wait()


def keeps(slot, child):
    return abs(slot // 6 - 2 - child // 2) > 1 or abs(slot % 6 - 2 - child % 2) > 1


def far_children(pairs, weight):
    low = lax.broadcasted_iota(I32, (8, 128), 1) < 64
    zero = jnp.zeros((8, 128), F32)
    sources, matrices = [], []
    for u, pair in pairs:
        rows = []
        for child in range(4):
            first, second = keeps(2 * u, child), keeps(2 * u + 1, child)
            if first and second:
                rows.append(pair)
            elif first:
                rows.append(jnp.where(low, pair, zero))
            elif second:
                rows.append(jnp.where(low, zero, pair))
            else:
                rows.append(zero)
        sources.append(jnp.concatenate(rows, axis=0).astype(BF16))
        matrices.append(jnp.concatenate([weight(child, u) for child in range(4)], axis=0))
    total = dot(jnp.concatenate(sources, axis=1), jnp.concatenate(matrices, axis=1), NT)
    owner = lax.broadcasted_iota(I32, (8, 256), 1) >> 6
    result = jnp.zeros((8, 256), F32)
    for child in range(4):
        result = result + jnp.where(owner == child, total[8 * child : 8 * child + 8], 0.0)
    return result


def window_mask(row, col, rows, cols, by_box):
    slot = lax.broadcasted_iota(I32, (8, 2304), 1) >> 6
    if by_box:
        box = slot >> 2
        box_row = (box * 11) >> 5
        slot_row = 2 * box_row + (slot & 1)
        slot_col = 2 * (box - 3 * box_row) + ((slot >> 1) & 1)
    else:
        slot_row = (slot * 43) >> 8
        slot_col = slot - 6 * slot_row
    source_row = slot_row + 2 * (row // 2) - 2
    source_col = slot_col + 2 * (col // 2) - 2
    inside = (source_row >= 0) & (source_row < rows) & (source_col >= 0) & (source_col < cols)
    apart = (jnp.abs(source_row - row) > 1) | (jnp.abs(source_col - col) > 1)
    return jnp.where(inside & apart, 1.0, 0.0)


def strip(step):
    return {-1: (2, 6, 2), 0: (2, 2, 4), 1: (4, 0, 2)}[step]


def main_kernel(
    grid_rows,
    grid_cols,
    values_ref,
    slot_ref,
    top_ref,
    basis_any,
    near_any,
    e0_any,
    e1_any,
    e2_any,
    e3_any,
    m0_any,
    m1_any,
    m2_any,
    m3_any,
    out_ref,
    inverse_ref,
    basis,
    near,
    e0,
    e1,
    e2,
    e3,
    m0,
    m1,
    m2,
    m3,
    m0_pairs,
    m1_pairs,
    w2,
    w3,
    w4,
    part_wide,
    part,
    e3_twice,
    e3_spread,
    top_matrix,
    fall,
    turn,
    lane_hot,
    mask2,
    mask3,
    mask4,
    halo,
    window,
    twos,
    threes,
    fours,
    pair_tiles,
    near_sum,
    far_zero,
    local_sem,
    block_send,
    block_recv,
    top_send,
    top_recv,
    three_send,
    three_recv,
    side_send,
    side_recv,
    halo_send,
    halo_recv,
    w3_send,
    w3_recv,
    cross_send,
    cross_recv,
    w4_send,
    w4_recv,
):
    i = lax.axis_index("gx")
    j = lax.axis_index("gy")
    pair_row, core = i // 2, i % 2
    patch, depth = j // 8, j % 8
    half = depth // 4
    own_pair = depth // 2

    def block_peer(a, b):
        return (2 * pair_row + (core + a) % 2, 8 * patch + (depth + b) % 8)

    def half_peer(a, b):
        return (2 * pair_row + (core + a) % 2, 8 * patch + 4 * half + (depth + b) % 4)

    def top_peer(a, b):
        return ((i + 2 * a) % grid_rows, (j + 8 * b + grid_cols) % grid_cols)

    def beside(a, b):
        return ((i + a + grid_rows) % grid_rows, (j + b + grid_cols) % grid_cols)

    def remote(source, target, send, recv, peer):
        return pltpu.make_async_remote_copy(
            src_ref=source,
            dst_ref=target,
            send_sem=send,
            recv_sem=recv,
            device_id=peer,
            device_id_type=MESH,
        )

    barrier = pltpu.get_barrier_semaphore()
    for a, b in TOP_PEERS:
        pl.semaphore_signal(barrier, 1, device_id=top_peer(a, b), device_id_type=MESH)
    for a, b in BLOCK_PEERS:
        pl.semaphore_signal(barrier, 1, device_id=block_peer(a, b), device_id_type=MESH)
    for a, b in BESIDE:
        pl.semaphore_signal(barrier, 1, device_id=beside(a, b), device_id_type=MESH)

    e3_own = e3_any.at[pl.ds(pair_row, 1), pl.ds(4 * patch, 4)]
    staged = [
        (basis_any, basis),
        (e0_any, e0),
        (e1_any, e1),
        (e2_any, e2),
        (m3_any, m3),
        (m2_any, m2),
        (e3_own, e3),
        (m1_any, m1),
        (m0_any, m0),
        (near_any, near),
    ]
    loads = [
        pltpu.make_async_copy(source, target, local_sem.at[n])
        for n, (source, target) in enumerate(staged)
    ]
    for load in loads:
        load.start()

    low = lax.broadcasted_iota(I32, (8, 128), 1) < 64

    def coefficients(product, leaf):
        level_zero = [dot(leaf[n].astype(BF16), basis[n // 4, n % 4], NT) for n in range(16)]
        level_one = []
        for p in range(4):
            pa, pb = p // 2, p % 2
            children = jnp.concatenate(
                [level_zero[4 * (2 * pa + c // 2) + 2 * pb + c % 2] for c in range(4)], axis=1
            ).astype(BF16)
            transfer = e0[2 * pa : 2 * pa + 2, 2 * pb : 2 * pb + 2].reshape(256, 64)
            level_one.append(dot(children, transfer, NN))
        for n in range(16):
            a, b = n // 4, n % 4
            coeffs = jnp.concatenate(
                [level_zero[n], level_one[2 * (a % 2) + b % 2]], axis=1
            )
            halo[product, 2 + a, 2 + b] = jnp.concatenate([leaf[n], coeffs], axis=0).astype(BF16)
        return level_one

    slots = slot_ref[0]
    slot_lane = lax.broadcasted_iota(I32, (128, 2048), 0) == (slots & 127)
    lane_hot[...] = jnp.where(slot_lane, 1.0, 0.0).astype(BF16)
    values = values_ref[0, 0].astype(F32)
    stacked = jnp.concatenate([values[:, 128 * s : 128 * s + 128] for s in range(16)], axis=0)
    candidates = dot(stacked.astype(BF16), lane_hot[...], NN)
    slot_block = jnp.broadcast_to(slots >> 7, (8, 2048))
    ordered = jnp.zeros((8, 2048), F32)
    for s in range(16):
        ordered = jnp.where(slot_block == s, candidates[8 * s : 8 * s + 8], ordered)

    for n in range(4):
        loads[n].wait()
    level_one = coefficients(0, [ordered[:, 128 * n : 128 * n + 128] for n in range(16)])
    level_two = dot(
        jnp.concatenate(level_one, axis=1).astype(BF16), e1[...].reshape(256, 64), NN
    )
    term = dot(level_two.astype(BF16), e2[0, 0], NN)
    window[0, core, depth] = jnp.concatenate(
        [term, level_two], axis=1
    )

    def block_copies(product):
        copies = []
        for n, (a, b) in enumerate(BLOCK_PEERS):
            copies.append(
                remote(
                    window.at[product, core, depth],
                    window.at[product, core, depth],
                    block_send.at[product, n],
                    block_recv.at[product, n],
                    block_peer(a, b),
                )
            )
        return copies

    def halo_copies(product):
        copies = []
        for n, (a, b) in enumerate(BESIDE):
            row_from, row_to, row_count = strip(a)
            col_from, col_to, col_count = strip(b)
            copies.append(
                remote(
                    halo.at[product, pl.ds(row_from, row_count), pl.ds(col_from, col_count)],
                    halo.at[product, pl.ds(row_to, row_count), pl.ds(col_to, col_count)],
                    halo_send.at[product, n],
                    halo_recv.at[product, n],
                    beside(a, b),
                )
            )
        return copies

    own_three = 2 * (i % 2) + j % 2
    own_four = 8 * (pair_row % 2) + 4 * (own_pair % 2) + own_three
    other_four = 8 - 8 * (pair_row % 2) + 4 * (own_pair % 2) + own_three
    next_three = 2 * (i % 2) + 1 - j % 2
    three_peers = [
        (2 * (i // 2) + (i + a) % 2, 2 * (j // 2) + (j + b) % 2) for a, b in ((1, 0), (0, 1))
    ]

    def w3_copy(n):
        return remote(
            w3.at[own_three], w3.at[own_three], w3_send.at[n], w3_recv.at[n], three_peers[n]
        )

    def w3_forward():
        return remote(
            w3.at[next_three], w3.at[next_three], w3_send.at[2], w3_recv.at[2], three_peers[0]
        )

    def cross_copies():
        return [
            remote(
                part, w4.at[own_four], cross_send.at[n], cross_recv.at[n], top_peer(a, 0)
            )
            for n, a in enumerate((2, 3 - 2 * (pair_row % 2)))
        ]

    def w4_copies():
        return [
            remote(
                w4.at[which],
                w4.at[which],
                w4_send.at[7 * m + n],
                w4_recv.at[7 * m + n],
                half_peer(a, b),
            )
            for m, which in enumerate((own_four, other_four))
            for n, (a, b) in enumerate(HALF_PEERS)
        ]

    def top_copies(product):
        return [
            remote(
                fours.at[product, pair_row, patch],
                fours.at[product, pair_row, patch],
                top_send.at[product, n],
                top_recv.at[product, n],
                top_peer(a, b),
            )
            for n, (a, b) in enumerate(TOP_PEERS)
        ]

    for t in range(16):
        part_wide[4 * (t // 4) : 4 * (t // 4) + 4, 64 * (t % 4) : 64 * (t % 4) + 64] = top_ref[
            0, 0, t
        ].astype(F32)
    part[...] = part_wide[...].astype(BF16)
    loads[4].wait()
    for u in range(18):
        w3[own_three, :, 128 * u : 128 * u + 128] = jnp.concatenate(
            [m3[0, 0, 2 * u], m3[0, 0, 2 * u + 1]], axis=1
        )
    loads[6].wait()
    coarse = e3[...].reshape(256, 64)
    first_half = lax.broadcasted_iota(I32, (256, 64), 0) < 128
    nothing = jnp.zeros((256, 64), F32)
    coarse = coarse.astype(F32)
    e3_twice[...] = jnp.concatenate(
        [jnp.where(first_half, coarse, nothing), jnp.where(first_half, nothing, coarse)], axis=1
    ).astype(BF16)
    loads[5].wait()

    pl.semaphore_wait(barrier, len(TOP_PEERS) + len(BLOCK_PEERS) + len(BESIDE))
    for copy in block_copies(0):
        copy.start()
    for copy in halo_copies(0):
        copy.start()
    for copy in cross_copies():
        copy.start()
    w3_copy(0).start()
    w3_copy(1).start()

    def set_up():
        loads[7].wait()
        for n in range(4):
            for u in range(18):
                m1_pairs[n, u] = jnp.concatenate(
                    [m1[n // 2, n % 2, 2 * u], m1[n // 2, n % 2, 2 * u + 1]], axis=1
                )
        loads[8].wait()

        def pack(n, inner):
            for u in range(18):
                m0_pairs[n, u] = jnp.concatenate(
                    [m0[n // 4, n % 4, 2 * u], m0[n // 4, n % 4, 2 * u + 1]], axis=1
                )
            return inner

        lax.fori_loop(0, 16, pack, 0)

    def set_up_more():
        for u in range(18):
            first = 12 * (u // 6) + u % 6
            w2[:, 128 * u : 128 * u + 128] = jnp.concatenate(
                [m2[0, 0, first], m2[0, 0, first + 6]], axis=1
            )
        mask2[...] = window_mask(i, j, grid_rows, grid_cols, True)
        mask3[...] = window_mask(i // 2, j // 2, grid_rows // 2, grid_cols // 2, False)
        top_box = lax.broadcasted_iota(I32, (8, 1024), 1) >> 6
        apart = (jnp.abs((top_box >> 3) - i // 4) > 1) | (jnp.abs((top_box & 7) - j // 4) > 1)
        mask4[...] = jnp.where(apart, 1.0, 0.0)
        spread_row = lax.broadcasted_iota(I32, (64, 256), 0)
        spread_col = lax.broadcasted_iota(I32, (64, 256), 1)
        chosen = spread_row == (spread_col >> 4) * 4 + (spread_col & 3)
        spread = dot(e3[0, own_pair], jnp.where(chosen, 1.0, 0.0).astype(BF16), NN)
        for q in range(4):
            e3_spread[q] = jnp.where(((spread_col >> 2) & 3) == q, spread, 0.0).astype(BF16)
        for p in range(4):
            pa, pb = p // 2, p % 2
            transfer = e0[2 * pa : 2 * pa + 2, 2 * pb : 2 * pb + 2].reshape(256, 64)
            two = dot(transfer, e1[pa, pb], NN)
            both = jnp.concatenate([dot(two.astype(BF16), e2[0, 0], NN), two], axis=1)
            for c in range(4):
                a, b = 2 * pa + c // 2, 2 * pb + c % 2
                rows = both[64 * c : 64 * c + 64].T.astype(BF16)
                n = 4 * a + b
                fall[:, 128 * n : 128 * n + 128] = dot(rows, basis[a, b], NN).astype(BF16)
        turn[...] = dot(fall[...], fall[...], NT).astype(BF16)

    def invert():
        slot_hot = lax.broadcasted_iota(I32, (16, 2048), 0) == (slot_ref[0] >> 7)
        position = lax.broadcasted_iota(I32, (16, 2048), 1)
        coded = jnp.concatenate(
            [
                jnp.where(slot_hot, (position >> 7).astype(F32), 0.0),
                jnp.where(slot_hot, (position & 127).astype(F32), 0.0),
            ],
            axis=0,
        ).astype(BF16)
        counted = dot(coded, lane_hot[...], NT)
        inverse_ref[...] = (counted[:16] * 128.0 + counted[16:]).astype(I32)

    def near_part(product, outside):
        for n in range(16):
            a, b = n // 4, n % 4
            places = [
                m
                for m in range(9)
                if outside
                != (0 <= a + m // 3 - 1 < 4 and 0 <= b + m % 3 - 1 < 4)
            ]
            if not places:
                continue
            sources = jnp.concatenate(
                [
                    halo[product, a + 1 + m // 3, b + 1 + m % 3].astype(F32)[:8]
                    for m in places
                ],
                axis=1,
            ).astype(BF16)
            blocks = jnp.concatenate([near[a, b, m] for m in places], axis=1)
            total = dot(sources, blocks, NT)
            near_sum[n] = near_sum[n] + total if outside else total

    def coeffs(product, a, b):
        return halo[product, a, b].astype(F32)[8:]

    def pair_part(product, outside):
        for a in range(8):
            for b in range(4):
                if outside != (2 <= a < 6 and 1 <= b < 3):
                    pair_tiles[a, b] = jnp.where(
                        low,
                        coeffs(product, a, 2 * b),
                        pltpu.roll(coeffs(product, a, 2 * b + 1), 64, 1),
                    )
        for p in range(4):
            pa, pb = p // 2, p % 2
            pairs = []
            for u in range(18):
                a, b = 2 * pa + u // 3, pb + u % 3
                if outside != (2 <= a < 6 and 1 <= b < 3):
                    pairs.append((u, pair_tiles[a, b]))
            total = far_children(
                pairs,
                lambda child, u: m0_pairs[4 * (2 * pa + child // 2) + 2 * pb + child % 2, u],
            )
            far_zero[p] = far_zero[p] + total if outside else total

    def interior(product):
        near_part(product, False)
        pair_part(product, False)

    def apply(product, carry):
        @pl.when(product == 0)
        def _():
            set_up_more()
            set_up()

        for copy in block_copies(product):
            copy.wait_recv()
        sums = []
        for b in range(4):
            tiles = [window[product, c // 2, 2 * b + c % 2] for c in range(4)]
            sums.append((tiles[0] + tiles[1]) + (tiles[2] + tiles[3]))
        rows = [
            jnp.where(low, sums[2 * h], pltpu.roll(sums[2 * h + 1], 64, 1)) for h in range(2)
        ]
        fours[product, pair_row, patch] = dot(
            jnp.concatenate(rows, axis=1).astype(BF16), e3_twice[...], NN
        )
        for copy in top_copies(product):
            copy.start()
        for h in range(2):
            threes[product, pair_row, 0, h] = rows[h]
        step = 1 - 2 * half
        three_copies = []
        for a in range(1, 4):
            three_copies.append((threes.at[product, pair_row, 0], threes.at[product, pair_row, 0], a, 0))
        for a in range(4):
            three_copies.append(
                (
                    threes.at[product, pair_row, 0, 1 - half],
                    threes.at[product, pair_row, 1, 1 - half],
                    a,
                    step,
                )
            )
        three_copies = [
            remote(
                source,
                target,
                three_send.at[product, n],
                three_recv.at[product, n],
                top_peer(a, b),
            )
            for n, (source, target, a, b) in enumerate(three_copies)
        ]
        for copy in three_copies:
            copy.start()
        @pl.when(product == 0)
        def _():
            for copy in cross_copies():
                copy.wait_recv()
            for copy in w4_copies():
                copy.start()

        for b in range(4):
            pieces = [
                jnp.where(
                    low,
                    pltpu.roll(window[product, 0, 2 * b + c], 64, 1),
                    window[product, 1, 2 * b + c],
                )
                for c in range(2)
            ]
            twos[product, 1, 1 + b] = jnp.concatenate(pieces, axis=0).astype(BF16)
        inner = pl.ds(1, 4)
        side_from, side_to = pl.ds(4 - 3 * half, 1), pl.ds(5 * half, 1)
        side_copies = [
            remote(
                twos.at[product, 1, source],
                twos.at[product, row, target],
                side_send.at[product, n],
                side_recv.at[product, n],
                top_peer(a, b),
            )
            for n, (row, source, target, a, b) in enumerate(
                (
                    (0, inner, inner, 1, 0),
                    (2, inner, inner, 3, 0),
                    (0, side_from, side_to, 1, step),
                    (1, side_from, side_to, 0, step),
                    (2, side_from, side_to, 3, step),
                )
            )
        ]
        for copy in side_copies:
            copy.start()

        @pl.when(product == 0)
        def _():
            loads[9].wait()
            interior(0)

        for copy in halo_copies(product):
            copy.wait_recv()
        blank = jnp.zeros((16, 128), BF16)

        def clear(cells):
            for a, b in cells:
                halo[product, a, b] = blank

        @pl.when(i == 0)
        def _():
            clear([(a, b) for a in (0, 1) for b in range(8)])

        @pl.when(i == grid_rows - 1)
        def _():
            clear([(a, b) for a in (6, 7) for b in range(8)])

        @pl.when(j == 0)
        def _():
            clear([(a, b) for a in range(8) for b in (0, 1)])

        @pl.when(j == grid_cols - 1)
        def _():
            clear([(a, b) for a in range(8) for b in (6, 7)])

        near_part(product, True)

        @pl.when(product == 0)
        def _():
            w3_copy(1).wait_recv()
            w3_forward().start()

        pair_part(product, True)
        one_pairs = []
        for u in range(18):
            a, b = (0, 1, 2, 3, 6, 7)[u // 3], (0, 2, 6)[u % 3]
            one_pairs.append(
                (
                    u,
                    jnp.where(
                        low,
                        pltpu.roll(coeffs(product, a, b), 64, 1),
                        coeffs(product, a, b + 1),
                    ),
                )
            )
        local_one = far_children(one_pairs, lambda child, u: m1_pairs[child, u])
        partly = [None] * 16
        for p in range(4):
            pa, pb = p // 2, p % 2
            transfer = e0[2 * pa : 2 * pa + 2, 2 * pb : 2 * pb + 2].reshape(256, 64)
            local_zero = far_zero[p] + dot(
                local_one[:, 64 * p : 64 * p + 64].astype(BF16), transfer, NT
            )
            for c in range(4):
                a, b = 2 * pa + c // 2, 2 * pb + c % 2
                partly[4 * a + b] = near_sum[4 * a + b] + dot(
                    local_zero[:, 64 * c : 64 * c + 64].astype(BF16), basis[a, b], NN
                )
        for n in range(16):
            near_sum[n] = partly[n]
        risen = dot(jnp.concatenate(partly, axis=1).astype(BF16), fall[...], NT)

        for copy in side_copies:
            copy.wait_recv()
        two_sources = []
        for u in range(18):
            if u % 2 == 0:
                tile = twos[product, u // 6, own_pair + (u // 2) % 3].astype(F32)
            two_sources.append(tile[8 * (u % 2) :][:8])
        two_sources = jnp.where(mask2[...] > 0.0, jnp.concatenate(two_sources, axis=1), 0.0)
        far_two = dot(two_sources.astype(BF16), w2[...], NT)

        @pl.when(product == 0)
        def _():
            w3_copy(0).wait_recv()
            w3_forward().wait_recv()

        for copy in three_copies:
            copy.wait_recv()
        three_parts = ((1 - half, 1 - half), (0, half), (half, 1 - half))
        three_sources = jnp.concatenate(
            [
                threes[product, (2 * (i // 4) + 2 + u // 3) % 4, side, part_half]
                for u in range(18)
                for side, part_half in (three_parts[u % 3],)
            ],
            axis=1,
        )
        three_sources = jnp.where(mask3[...] > 0.0, three_sources, 0.0)
        far_three = dot(three_sources.astype(BF16), w3[...].reshape(64, 2304), NT)
        far_both = jnp.concatenate([far_three, far_two], axis=1)

        @pl.when(product == 0)
        def _():
            for copy in w4_copies():
                copy.wait_recv()
            rows_four = w4[...].reshape(256, 256)
            for q in range(4):
                top_matrix[0:64, 256 * q : 256 * q + 256] = dot(
                    e3_spread[q], rows_four, NN
                ).astype(BF16)
                top_matrix[64:128, 256 * q : 256 * q + 256] = jnp.zeros((64, 256), BF16)

        for copy in block_copies(product) + halo_copies(product) + three_copies + side_copies:
            copy.wait_send()
        for copy in top_copies(product):
            copy.wait_recv()
        four_sources = jnp.concatenate(
            [
                fours[product, 2 * (t // 4), t % 4] + fours[product, 2 * (t // 4) + 1, t % 4]
                for t in range(8)
            ],
            axis=1,
        )
        four_sources = jnp.where(mask4[...] > 0.0, four_sources, 0.0)
        falling = (far_both + dot(four_sources.astype(BF16), top_matrix[...], NT)).astype(BF16)

        @pl.when(product == 0)
        def _():
            window[1, core, depth] = risen + dot(
                falling, turn[...], NN
            )
            for copy in block_copies(1):
                copy.start()

        fallen = dot(falling, fall[...], NN)
        results = [near_sum[n] + fallen[:, 128 * n : 128 * n + 128] for n in range(16)]
        for n in range(16):
            out_ref[product, n] = results[n]

        @pl.when(product == 0)
        def _():
            coefficients(1, results)
            for copy in halo_copies(1):
                copy.start()
            interior(1)
            invert()

        return carry

    lax.fori_loop(0, 2, apply, 0)
    for product in range(2):
        for copy in top_copies(product):
            copy.wait_send()
    for copy in [w3_copy(0), w3_copy(1), w3_forward()] + cross_copies() + w4_copies():
        copy.wait_send()


def local(
    grid_rows,
    grid_cols,
    values,
    point_slot,
    leaf_basis,
    near_blocks,
    transfer_leaf,
    transfer_mid,
    transfer_dev,
    transfer_coarse,
    coupling_leaf,
    coupling_mid,
    coupling_dev,
    coupling_coarse,
    coupling_top,
):
    whole = pl.BlockSpec(memory_space=pltpu.VMEM)
    left = pl.BlockSpec(memory_space=pl.ANY)
    dma = pltpu.SemaphoreType.DMA
    params = pltpu.CompilerParams(vmem_limit_bytes=VMEM_LIMIT)
    products, inverse = pl.pallas_call(
        functools.partial(main_kernel, grid_rows, grid_cols),
        out_shape=(
            jax.ShapeDtypeStruct((2, 16, 8, 128), F32),
            jax.ShapeDtypeStruct((16, 128), I32),
        ),
        in_specs=[whole] * 3 + [left] * LOCAL_ARRAYS,
        out_specs=(whole,) * 2,
        scratch_shapes=[
            pltpu.VMEM((4, 4, 64, 128), BF16),
            pltpu.VMEM((4, 4, 9, 128, 128), BF16),
            pltpu.VMEM((4, 4, 64, 64), BF16),
            pltpu.VMEM((2, 2, 64, 64), BF16),
            pltpu.VMEM((1, 1, 64, 64), BF16),
            pltpu.VMEM((1, 4, 64, 64), BF16),
            pltpu.VMEM((4, 4, 36, 64, 64), BF16),
            pltpu.VMEM((2, 2, 36, 64, 64), BF16),
            pltpu.VMEM((1, 1, 36, 64, 64), BF16),
            pltpu.VMEM((1, 1, 36, 16, 64), BF16),
            pltpu.VMEM((16, 18, 64, 128), BF16),
            pltpu.VMEM((4, 18, 64, 128), BF16),
            pltpu.VMEM((64, 2304), BF16),
            pltpu.VMEM((4, 16, 2304), BF16),
            pltpu.VMEM((16, 16, 256), BF16),
            pltpu.VMEM((16, 256), F32),
            pltpu.VMEM((16, 256), BF16),
            pltpu.VMEM((256, 128), BF16),
            pltpu.VMEM((4, 64, 256), BF16),
            pltpu.VMEM((128, 1024), BF16),
            pltpu.VMEM((128, 2048), BF16),
            pltpu.VMEM((128, 128), BF16),
            pltpu.VMEM((128, 2048), BF16),
            pltpu.VMEM((8, 2304), F32),
            pltpu.VMEM((8, 2304), F32),
            pltpu.VMEM((8, 1024), F32),
            pltpu.VMEM((2, 8, 8, 16, 128), BF16),
            pltpu.VMEM((2, 2, 8, 8, 128), F32),
            pltpu.VMEM((2, 3, 6, 16, 128), BF16),
            pltpu.VMEM((2, 4, 2, 2, 8, 128), F32),
            pltpu.VMEM((2, 4, 4, 8, 128), F32),
            pltpu.VMEM((8, 4, 8, 128), F32),
            pltpu.VMEM((16, 8, 128), F32),
            pltpu.VMEM((4, 8, 256), F32),
            dma((LOCAL_ARRAYS,)),
            dma((2, 15)),
            dma((2, 15)),
            dma((2, 15)),
            dma((2, 15)),
            dma((2, 7)),
            dma((2, 7)),
            dma((2, 5)),
            dma((2, 5)),
            dma((2, 8)),
            dma((2, 8)),
            dma((3,)),
            dma((3,)),
            dma((2,)),
            dma((2,)),
            dma((14,)),
            dma((14,)),
        ],
        compiler_params=pltpu.CompilerParams(
            collective_id=0, has_side_effects=True, vmem_limit_bytes=VMEM_LIMIT
        ),
    )(
        jnp.transpose(values, (1, 2, 0, 3)),
        point_slot,
        coupling_top,
        jnp.swapaxes(leaf_basis, 2, 3),
        near_blocks,
        transfer_leaf,
        transfer_mid,
        transfer_dev,
        transfer_coarse,
        coupling_leaf,
        coupling_mid,
        coupling_dev,
        coupling_coarse,
    )
    placed = jax.ShapeDtypeStruct(values.shape, F32)
    return pl.pallas_call(
        place_kernel,
        out_shape=(placed, placed),
        in_specs=[left] * 2,
        out_specs=(left,) * 2,
        scratch_shapes=[
            pltpu.VMEM((2, 16, 8, 128), F32),
            pltpu.VMEM((16, 128), I32),
            pltpu.VMEM((2, 8, 1, 1, 2048), F32),
            dma((3,)),
            dma((2,)),
        ],
        compiler_params=params,
    )(products, inverse)


def solution(mesh):
    placed = (
        P(None, "gx", "gy", None),
        P("gx", "gy", None),
        P("gx", "gy", None, None),
        P("gx", "gy", None, None, None),
        P("gx", "gy", None, None),
        P("gx", "gy", None, None),
        P("gx", "gy", None, None),
        P(),
        P("gx", "gy", None, None, None),
        P("gx", "gy", None, None, None),
        P("gx", "gy", None, None, None),
        P("gx", "gy", None, None, None),
        P("gx", "gy", None, None, None),
    )
    return jax.shard_map(
        functools.partial(local, mesh.shape["gx"], mesh.shape["gy"]),
        mesh=mesh,
        in_specs=placed,
        out_specs=(P(None, "gx", "gy", None), P(None, "gx", "gy", None)),
        check_vma=False,
    )
```

```python
import functools

import jax
import jax.numpy as jnp
from jax import lax
from jax.experimental import pallas as pl
from jax.experimental.pallas import tpu as pltpu
from jax.sharding import PartitionSpec as P

F32 = jnp.float32
BF16 = jnp.bfloat16
I32 = jnp.int32
MESH = pl.DeviceIdType.MESH
NN = (((1,), (0,)), ((), ()))
NT = (((1,), (1,)), ((), ()))
VMEM_LIMIT = 56 * 2**20

BLOCK_PEERS = [(a, b) for b in (4, 3, 5, 2, 6, 1, 7) for a in (1, 0)] + [(1, 0)]
TOP_PEERS = [(2, 2), (2, 1), (2, 3), (1, 2), (3, 2), (1, 1), (1, 3), (3, 1), (3, 3)] + [
    (2, 0),
    (0, 2),
    (1, 0),
    (3, 0),
    (0, 1),
    (0, 3),
]
HALF_PEERS = [(a, b) for a in range(2) for b in range(4) if a or b]
BESIDE = [(a, b) for a in (-1, 0, 1) for b in (-1, 0, 1) if a or b]
LOCAL_ARRAYS = 10


def dot(left, right, dims):
    return lax.dot_general(left, right, dims, preferred_element_type=F32)


def permute(blocks, index_row):
    index = jnp.broadcast_to(index_row, (8, 128))
    lane = index & 127
    source = index >> 7
    result = None
    for block, piece in enumerate(blocks):
        taken = jnp.take_along_axis(piece, lane, axis=1, mode="promise_in_bounds")
        result = taken if result is None else jnp.where(source == block, taken, result)
    return result


def place_kernel(
    ordered_any,
    inverse_any,
    first_any,
    second_any,
    ordered,
    inverse,
    placed,
    load_sem,
    store_sem,
):
    loads = [
        pltpu.make_async_copy(inverse_any, inverse, load_sem.at[2]),
        pltpu.make_async_copy(ordered_any.at[0], ordered.at[0], load_sem.at[0]),
        pltpu.make_async_copy(ordered_any.at[1], ordered.at[1], load_sem.at[1]),
    ]
    stores = [
        pltpu.make_async_copy(placed.at[0], first_any, store_sem.at[0]),
        pltpu.make_async_copy(placed.at[1], second_any, store_sem.at[1]),
    ]
    for load in loads:
        load.start()
    loads[0].wait()
    for which in range(2):
        loads[1 + which].wait()
        pieces = [ordered[which, s] for s in range(16)]
        for m in range(16):
            result = permute(pieces, inverse[m : m + 1])
            for r in range(8):
                placed[which, r, 0, 0:1, 128 * m : 128 * m + 128] = result[r : r + 1]
        stores[which].start()
    for store in stores:
        store.wait()


def keeps(slot, child):
    return abs(slot // 6 - 2 - child // 2) > 1 or abs(slot % 6 - 2 - child % 2) > 1


def far_children(pairs, weight):
    low = lax.broadcasted_iota(I32, (8, 128), 1) < 64
    zero = jnp.zeros((8, 128), F32)
    sources, matrices = [], []
    for u, pair in pairs:
        rows = []
        for child in range(4):
            first, second = keeps(2 * u, child), keeps(2 * u + 1, child)
            if first and second:
                rows.append(pair)
            elif first:
                rows.append(jnp.where(low, pair, zero))
            elif second:
                rows.append(jnp.where(low, zero, pair))
            else:
                rows.append(zero)
        sources.append(jnp.concatenate(rows, axis=0).astype(BF16))
        matrices.append(jnp.concatenate([weight(child, u) for child in range(4)], axis=0))
    total = dot(jnp.concatenate(sources, axis=1), jnp.concatenate(matrices, axis=1), NT)
    owner = lax.broadcasted_iota(I32, (8, 256), 1) >> 6
    result = jnp.zeros((8, 256), F32)
    for child in range(4):
        result = result + jnp.where(owner == child, total[8 * child : 8 * child + 8], 0.0)
    return result


def window_mask(row, col, rows, cols, by_box):
    slot = lax.broadcasted_iota(I32, (8, 2304), 1) >> 6
    if by_box:
        box = slot >> 2
        box_row = (box * 11) >> 5
        slot_row = 2 * box_row + (slot & 1)
        slot_col = 2 * (box - 3 * box_row) + ((slot >> 1) & 1)
    else:
        slot_row = (slot * 43) >> 8
        slot_col = slot - 6 * slot_row
    source_row = slot_row + 2 * (row // 2) - 2
    source_col = slot_col + 2 * (col // 2) - 2
    inside = (source_row >= 0) & (source_row < rows) & (source_col >= 0) & (source_col < cols)
    apart = (jnp.abs(source_row - row) > 1) | (jnp.abs(source_col - col) > 1)
    return jnp.where(inside & apart, 1.0, 0.0)


def strip(step):
    return {-1: (2, 6, 2), 0: (2, 2, 4), 1: (4, 0, 2)}[step]


def main_kernel(
    grid_rows,
    grid_cols,
    values_ref,
    slot_ref,
    top_ref,
    basis_any,
    near_any,
    e0_any,
    e1_any,
    e2_any,
    e3_any,
    m0_any,
    m1_any,
    m2_any,
    m3_any,
    out_ref,
    inverse_ref,
    basis,
    near,
    e0,
    e1,
    e2,
    e3,
    m0,
    m1,
    m2,
    m3,
    m0_pairs,
    m1_pairs,
    w2,
    w3,
    w4,
    part_wide,
    part,
    e3_twice,
    e3_spread,
    top_matrix,
    fall,
    turn,
    lane_hot,
    mask2,
    mask3,
    mask4,
    halo,
    window,
    twos,
    threes,
    fours,
    pair_tiles,
    near_sum,
    far_zero,
    local_sem,
    block_send,
    block_recv,
    top_send,
    top_recv,
    three_send,
    three_recv,
    side_send,
    side_recv,
    halo_send,
    halo_recv,
    w3_send,
    w3_recv,
    cross_send,
    cross_recv,
    w4_send,
    w4_recv,
):
    i = lax.axis_index("gx")
    j = lax.axis_index("gy")
    pair_row, core = i // 2, i % 2
    patch, depth = j // 8, j % 8
    half = depth // 4
    own_pair = depth // 2

    def block_peer(a, b):
        return (2 * pair_row + (core + a) % 2, 8 * patch + (depth + b) % 8)

    def half_peer(a, b):
        return (2 * pair_row + (core + a) % 2, 8 * patch + 4 * half + (depth + b) % 4)

    def top_peer(a, b):
        return ((i + 2 * a) % grid_rows, (j + 8 * b + grid_cols) % grid_cols)

    def beside(a, b):
        return ((i + a + grid_rows) % grid_rows, (j + b + grid_cols) % grid_cols)

    def remote(source, target, send, recv, peer):
        return pltpu.make_async_remote_copy(
            src_ref=source,
            dst_ref=target,
            send_sem=send,
            recv_sem=recv,
            device_id=peer,
            device_id_type=MESH,
        )

    barrier = pltpu.get_barrier_semaphore()
    for a, b in BESIDE:
        pl.semaphore_signal(barrier, 1, device_id=beside(a, b), device_id_type=MESH)
    for a, b in TOP_PEERS:
        pl.semaphore_signal(barrier, 1, device_id=top_peer(a, b), device_id_type=MESH)
    for a, b in BLOCK_PEERS:
        pl.semaphore_signal(barrier, 1, device_id=block_peer(a, b), device_id_type=MESH)

    e3_own = e3_any.at[pl.ds(pair_row, 1), pl.ds(4 * patch, 4)]
    staged = [
        (basis_any, basis),
        (e0_any, e0),
        (e1_any, e1),
        (e2_any, e2),
        (m3_any, m3),
        (m2_any, m2),
        (e3_own, e3),
        (m1_any, m1),
        (m0_any, m0),
        (near_any, near),
    ]
    loads = [
        pltpu.make_async_copy(source, target, local_sem.at[n])
        for n, (source, target) in enumerate(staged)
    ]
    for load in loads:
        load.start()

    low = lax.broadcasted_iota(I32, (8, 128), 1) < 64

    def coefficients(product, leaf):
        level_zero = [dot(leaf[n].astype(BF16), basis[n // 4, n % 4], NT) for n in range(16)]
        level_one = []
        for p in range(4):
            pa, pb = p // 2, p % 2
            children = jnp.concatenate(
                [level_zero[4 * (2 * pa + c // 2) + 2 * pb + c % 2] for c in range(4)], axis=1
            ).astype(BF16)
            transfer = e0[2 * pa : 2 * pa + 2, 2 * pb : 2 * pb + 2].reshape(256, 64)
            level_one.append(dot(children, transfer, NN))
        for n in range(16):
            a, b = n // 4, n % 4
            coeffs = jnp.concatenate(
                [level_zero[n], level_one[2 * (a % 2) + b % 2]], axis=1
            )
            halo[product, 2 + a, 2 + b] = jnp.concatenate([leaf[n], coeffs], axis=0).astype(BF16)
        return level_one

    slots = slot_ref[0]
    slot_lane = lax.broadcasted_iota(I32, (128, 2048), 0) == (slots & 127)
    lane_hot[...] = jnp.where(slot_lane, 1.0, 0.0).astype(BF16)
    values = values_ref[0, 0].astype(F32)
    stacked = jnp.concatenate([values[:, 128 * s : 128 * s + 128] for s in range(16)], axis=0)
    candidates = dot(stacked.astype(BF16), lane_hot[...], NN)
    slot_block = jnp.broadcast_to(slots >> 7, (8, 2048))
    ordered = jnp.zeros((8, 2048), F32)
    for s in range(16):
        ordered = jnp.where(slot_block == s, candidates[8 * s : 8 * s + 8], ordered)

    for n in range(4):
        loads[n].wait()
    level_one = coefficients(0, [ordered[:, 128 * n : 128 * n + 128] for n in range(16)])
    level_two = dot(
        jnp.concatenate(level_one, axis=1).astype(BF16), e1[...].reshape(256, 64), NN
    )
    term = dot(level_two.astype(BF16), e2[0, 0], NN)
    window[0, core, depth] = jnp.concatenate(
        [term, level_two], axis=1
    )

    def block_copies(product):
        copies = []
        for n, (a, b) in enumerate(BLOCK_PEERS):
            copies.append(
                remote(
                    window.at[product, core, depth],
                    window.at[product, core, depth],
                    block_send.at[product, n],
                    block_recv.at[product, n],
                    block_peer(a, b),
                )
            )
        return copies

    def halo_copies(product):
        copies = []
        for n, (a, b) in enumerate(BESIDE):
            row_from, row_to, row_count = strip(a)
            col_from, col_to, col_count = strip(b)
            copies.append(
                remote(
                    halo.at[product, pl.ds(row_from, row_count), pl.ds(col_from, col_count)],
                    halo.at[product, pl.ds(row_to, row_count), pl.ds(col_to, col_count)],
                    halo_send.at[product, n],
                    halo_recv.at[product, n],
                    beside(a, b),
                )
            )
        return copies

    own_three = 2 * (i % 2) + j % 2
    own_four = 8 * (pair_row % 2) + 4 * (own_pair % 2) + own_three
    other_four = 8 - 8 * (pair_row % 2) + 4 * (own_pair % 2) + own_three
    next_three = 2 * (i % 2) + 1 - j % 2
    three_peers = [
        (2 * (i // 2) + (i + a) % 2, 2 * (j // 2) + (j + b) % 2) for a, b in ((1, 0), (0, 1))
    ]

    def w3_copy(n):
        return remote(
            w3.at[own_three], w3.at[own_three], w3_send.at[n], w3_recv.at[n], three_peers[n]
        )

    def w3_forward():
        return remote(
            w3.at[next_three], w3.at[next_three], w3_send.at[2], w3_recv.at[2], three_peers[0]
        )

    def cross_copies():
        return [
            remote(
                part, w4.at[own_four], cross_send.at[n], cross_recv.at[n], top_peer(a, 0)
            )
            for n, a in enumerate((2, 3 - 2 * (pair_row % 2)))
        ]

    def w4_copies():
        return [
            remote(
                w4.at[which],
                w4.at[which],
                w4_send.at[7 * m + n],
                w4_recv.at[7 * m + n],
                half_peer(a, b),
            )
            for m, which in enumerate((own_four, other_four))
            for n, (a, b) in enumerate(HALF_PEERS)
        ]

    def top_copies(product):
        return [
            remote(
                fours.at[product, pair_row, patch],
                fours.at[product, pair_row, patch],
                top_send.at[product, n],
                top_recv.at[product, n],
                top_peer(a, b),
            )
            for n, (a, b) in enumerate(TOP_PEERS)
        ]

    pl.semaphore_wait(barrier, len(TOP_PEERS) + len(BLOCK_PEERS) + len(BESIDE))
    for copy in block_copies(0):
        copy.start()
    for copy in halo_copies(0):
        copy.start()
    for t in range(16):
        part_wide[4 * (t // 4) : 4 * (t // 4) + 4, 64 * (t % 4) : 64 * (t % 4) + 64] = top_ref[
            0, 0, t
        ].astype(F32)
    part[...] = part_wide[...].astype(BF16)
    loads[4].wait()
    for u in range(18):
        w3[own_three, :, 128 * u : 128 * u + 128] = jnp.concatenate(
            [m3[0, 0, 2 * u], m3[0, 0, 2 * u + 1]], axis=1
        )
    loads[6].wait()
    coarse = e3[...].reshape(256, 64)
    first_half = lax.broadcasted_iota(I32, (256, 64), 0) < 128
    nothing = jnp.zeros((256, 64), F32)
    coarse = coarse.astype(F32)
    e3_twice[...] = jnp.concatenate(
        [jnp.where(first_half, coarse, nothing), jnp.where(first_half, nothing, coarse)], axis=1
    ).astype(BF16)
    loads[5].wait()

    for copy in cross_copies():
        copy.start()
    w3_copy(0).start()
    w3_copy(1).start()

    def set_up():
        loads[7].wait()
        for n in range(4):
            for u in range(18):
                m1_pairs[n, u] = jnp.concatenate(
                    [m1[n // 2, n % 2, 2 * u], m1[n // 2, n % 2, 2 * u + 1]], axis=1
                )
        loads[8].wait()

        def pack(n, inner):
            for u in range(18):
                m0_pairs[n, u] = jnp.concatenate(
                    [m0[n // 4, n % 4, 2 * u], m0[n // 4, n % 4, 2 * u + 1]], axis=1
                )
            return inner

        lax.fori_loop(0, 16, pack, 0)

    def set_up_more():
        for u in range(18):
            first = 12 * (u // 6) + u % 6
            w2[:, 128 * u : 128 * u + 128] = jnp.concatenate(
                [m2[0, 0, first], m2[0, 0, first + 6]], axis=1
            )
        mask2[...] = window_mask(i, j, grid_rows, grid_cols, True)
        mask3[...] = window_mask(i // 2, j // 2, grid_rows // 2, grid_cols // 2, False)
        top_box = lax.broadcasted_iota(I32, (8, 1024), 1) >> 6
        apart = (jnp.abs((top_box >> 3) - i // 4) > 1) | (jnp.abs((top_box & 7) - j // 4) > 1)
        mask4[...] = jnp.where(apart, 1.0, 0.0)
        spread_row = lax.broadcasted_iota(I32, (64, 256), 0)
        spread_col = lax.broadcasted_iota(I32, (64, 256), 1)
        chosen = spread_row == (spread_col >> 4) * 4 + (spread_col & 3)
        spread = dot(e3[0, own_pair], jnp.where(chosen, 1.0, 0.0).astype(BF16), NN)
        for q in range(4):
            e3_spread[q] = jnp.where(((spread_col >> 2) & 3) == q, spread, 0.0).astype(BF16)
        for p in range(4):
            pa, pb = p // 2, p % 2
            transfer = e0[2 * pa : 2 * pa + 2, 2 * pb : 2 * pb + 2].reshape(256, 64)
            two = dot(transfer, e1[pa, pb], NN)
            both = jnp.concatenate([dot(two.astype(BF16), e2[0, 0], NN), two], axis=1)
            for c in range(4):
                a, b = 2 * pa + c // 2, 2 * pb + c % 2
                rows = both[64 * c : 64 * c + 64].T.astype(BF16)
                n = 4 * a + b
                fall[:, 128 * n : 128 * n + 128] = dot(rows, basis[a, b], NN).astype(BF16)
        turn[...] = dot(fall[...], fall[...], NT).astype(BF16)

    def invert():
        slot_hot = lax.broadcasted_iota(I32, (16, 2048), 0) == (slot_ref[0] >> 7)
        position = lax.broadcasted_iota(I32, (16, 2048), 1)
        coded = jnp.concatenate(
            [
                jnp.where(slot_hot, (position >> 7).astype(F32), 0.0),
                jnp.where(slot_hot, (position & 127).astype(F32), 0.0),
            ],
            axis=0,
        ).astype(BF16)
        counted = dot(coded, lane_hot[...], NT)
        inverse_ref[...] = (counted[:16] * 128.0 + counted[16:]).astype(I32)

    def near_part(product, outside):
        for n in range(16):
            a, b = n // 4, n % 4
            places = [
                m
                for m in range(9)
                if outside
                != (0 <= a + m // 3 - 1 < 4 and 0 <= b + m % 3 - 1 < 4)
            ]
            if not places:
                continue
            sources = jnp.concatenate(
                [
                    halo[product, a + 1 + m // 3, b + 1 + m % 3].astype(F32)[:8]
                    for m in places
                ],
                axis=1,
            ).astype(BF16)
            blocks = jnp.concatenate([near[a, b, m] for m in places], axis=1)
            total = dot(sources, blocks, NT)
            near_sum[n] = near_sum[n] + total if outside else total

    def coeffs(product, a, b):
        return halo[product, a, b].astype(F32)[8:]

    def pair_part(product, outside):
        for a in range(8):
            for b in range(4):
                if outside != (2 <= a < 6 and 1 <= b < 3):
                    pair_tiles[a, b] = jnp.where(
                        low,
                        coeffs(product, a, 2 * b),
                        pltpu.roll(coeffs(product, a, 2 * b + 1), 64, 1),
                    )
        for p in range(4):
            pa, pb = p // 2, p % 2
            pairs = []
            for u in range(18):
                a, b = 2 * pa + u // 3, pb + u % 3
                if outside != (2 <= a < 6 and 1 <= b < 3):
                    pairs.append((u, pair_tiles[a, b]))
            total = far_children(
                pairs,
                lambda child, u: m0_pairs[4 * (2 * pa + child // 2) + 2 * pb + child % 2, u],
            )
            far_zero[p] = far_zero[p] + total if outside else total

    def interior(product):
        near_part(product, False)
        pair_part(product, False)

    def apply(product, carry):
        @pl.when(product == 0)
        def _():
            set_up_more()
            set_up()

        for copy in block_copies(product):
            copy.wait_recv()
        sums = []
        for b in range(4):
            tiles = [window[product, c // 2, 2 * b + c % 2] for c in range(4)]
            sums.append((tiles[0] + tiles[1]) + (tiles[2] + tiles[3]))
        rows = [
            jnp.where(low, sums[2 * h], pltpu.roll(sums[2 * h + 1], 64, 1)) for h in range(2)
        ]
        fours[product, pair_row, patch] = dot(
            jnp.concatenate(rows, axis=1).astype(BF16), e3_twice[...], NN
        )
        for copy in top_copies(product):
            copy.start()
        for h in range(2):
            threes[product, pair_row, 0, h] = rows[h]
        step = 1 - 2 * half
        three_copies = []
        for a in range(1, 4):
            three_copies.append((threes.at[product, pair_row, 0], threes.at[product, pair_row, 0], a, 0))
        for a in range(4):
            three_copies.append(
                (
                    threes.at[product, pair_row, 0, 1 - half],
                    threes.at[product, pair_row, 1, 1 - half],
                    a,
                    step,
                )
            )
        three_copies = [
            remote(
                source,
                target,
                three_send.at[product, n],
                three_recv.at[product, n],
                top_peer(a, b),
            )
            for n, (source, target, a, b) in enumerate(three_copies)
        ]
        for copy in three_copies:
            copy.start()
        @pl.when(product == 0)
        def _():
            for copy in cross_copies():
                copy.wait_recv()
            for copy in w4_copies():
                copy.start()

        for b in range(4):
            pieces = [
                jnp.where(
                    low,
                    pltpu.roll(window[product, 0, 2 * b + c], 64, 1),
                    window[product, 1, 2 * b + c],
                )
                for c in range(2)
            ]
            twos[product, 1, 1 + b] = jnp.concatenate(pieces, axis=0).astype(BF16)
        inner = pl.ds(1, 4)
        side_from, side_to = pl.ds(4 - 3 * half, 1), pl.ds(5 * half, 1)
        side_copies = [
            remote(
                twos.at[product, 1, source],
                twos.at[product, row, target],
                side_send.at[product, n],
                side_recv.at[product, n],
                top_peer(a, b),
            )
            for n, (row, source, target, a, b) in enumerate(
                (
                    (0, inner, inner, 1, 0),
                    (2, inner, inner, 3, 0),
                    (0, side_from, side_to, 1, step),
                    (1, side_from, side_to, 0, step),
                    (2, side_from, side_to, 3, step),
                )
            )
        ]
        for copy in side_copies:
            copy.start()

        @pl.when(product == 0)
        def _():
            loads[9].wait()
            interior(0)

        for copy in halo_copies(product):
            copy.wait_recv()
        blank = jnp.zeros((16, 128), BF16)

        def clear(cells):
            for a, b in cells:
                halo[product, a, b] = blank

        @pl.when(i == 0)
        def _():
            clear([(a, b) for a in (0, 1) for b in range(8)])

        @pl.when(i == grid_rows - 1)
        def _():
            clear([(a, b) for a in (6, 7) for b in range(8)])

        @pl.when(j == 0)
        def _():
            clear([(a, b) for a in range(8) for b in (0, 1)])

        @pl.when(j == grid_cols - 1)
        def _():
            clear([(a, b) for a in range(8) for b in (6, 7)])

        near_part(product, True)

        @pl.when(product == 0)
        def _():
            w3_copy(1).wait_recv()
            w3_forward().start()

        pair_part(product, True)
        one_pairs = []
        for u in range(18):
            a, b = (0, 1, 2, 3, 6, 7)[u // 3], (0, 2, 6)[u % 3]
            one_pairs.append(
                (
                    u,
                    jnp.where(
                        low,
                        pltpu.roll(coeffs(product, a, b), 64, 1),
                        coeffs(product, a, b + 1),
                    ),
                )
            )
        local_one = far_children(one_pairs, lambda child, u: m1_pairs[child, u])
        partly = [None] * 16
        for p in range(4):
            pa, pb = p // 2, p % 2
            transfer = e0[2 * pa : 2 * pa + 2, 2 * pb : 2 * pb + 2].reshape(256, 64)
            local_zero = far_zero[p] + dot(
                local_one[:, 64 * p : 64 * p + 64].astype(BF16), transfer, NT
            )
            for c in range(4):
                a, b = 2 * pa + c // 2, 2 * pb + c % 2
                partly[4 * a + b] = near_sum[4 * a + b] + dot(
                    local_zero[:, 64 * c : 64 * c + 64].astype(BF16), basis[a, b], NN
                )
        for n in range(16):
            near_sum[n] = partly[n]
        risen = dot(jnp.concatenate(partly, axis=1).astype(BF16), fall[...], NT)

        for copy in side_copies:
            copy.wait_recv()
        two_sources = []
        for u in range(18):
            if u % 2 == 0:
                tile = twos[product, u // 6, own_pair + (u // 2) % 3].astype(F32)
            two_sources.append(tile[8 * (u % 2) :][:8])
        two_sources = jnp.where(mask2[...] > 0.0, jnp.concatenate(two_sources, axis=1), 0.0)
        far_two = dot(two_sources.astype(BF16), w2[...], NT)

        @pl.when(product == 0)
        def _():
            w3_copy(0).wait_recv()
            w3_forward().wait_recv()

        for copy in three_copies:
            copy.wait_recv()
        three_parts = ((1 - half, 1 - half), (0, half), (half, 1 - half))
        three_sources = jnp.concatenate(
            [
                threes[product, (2 * (i // 4) + 2 + u // 3) % 4, side, part_half]
                for u in range(18)
                for side, part_half in (three_parts[u % 3],)
            ],
            axis=1,
        )
        three_sources = jnp.where(mask3[...] > 0.0, three_sources, 0.0)
        far_three = dot(three_sources.astype(BF16), w3[...].reshape(64, 2304), NT)
        far_both = jnp.concatenate([far_three, far_two], axis=1)

        @pl.when(product == 0)
        def _():
            for copy in w4_copies():
                copy.wait_recv()
            rows_four = w4[...].reshape(256, 256)
            for q in range(4):
                top_matrix[0:64, 256 * q : 256 * q + 256] = dot(
                    e3_spread[q], rows_four, NN
                ).astype(BF16)
                top_matrix[64:128, 256 * q : 256 * q + 256] = jnp.zeros((64, 256), BF16)

        for copy in block_copies(product) + halo_copies(product) + three_copies + side_copies:
            copy.wait_send()
        for copy in top_copies(product):
            copy.wait_recv()
        four_sources = jnp.concatenate(
            [
                fours[product, 2 * (t // 4), t % 4] + fours[product, 2 * (t // 4) + 1, t % 4]
                for t in range(8)
            ],
            axis=1,
        )
        four_sources = jnp.where(mask4[...] > 0.0, four_sources, 0.0)
        falling = (far_both + dot(four_sources.astype(BF16), top_matrix[...], NT)).astype(BF16)

        @pl.when(product == 0)
        def _():
            window[1, core, depth] = risen + dot(
                falling, turn[...], NN
            )
            for copy in block_copies(1):
                copy.start()

        fallen = dot(falling, fall[...], NN)
        results = [near_sum[n] + fallen[:, 128 * n : 128 * n + 128] for n in range(16)]
        for n in range(16):
            out_ref[product, n] = results[n]

        @pl.when(product == 0)
        def _():
            coefficients(1, results)
            for copy in halo_copies(1):
                copy.start()
            interior(1)
            invert()

        return carry

    lax.fori_loop(0, 2, apply, 0)
    for product in range(2):
        for copy in top_copies(product):
            copy.wait_send()
    for copy in [w3_copy(0), w3_copy(1), w3_forward()] + cross_copies() + w4_copies():
        copy.wait_send()


def local(
    grid_rows,
    grid_cols,
    values,
    point_slot,
    leaf_basis,
    near_blocks,
    transfer_leaf,
    transfer_mid,
    transfer_dev,
    transfer_coarse,
    coupling_leaf,
    coupling_mid,
    coupling_dev,
    coupling_coarse,
    coupling_top,
):
    whole = pl.BlockSpec(memory_space=pltpu.VMEM)
    left = pl.BlockSpec(memory_space=pl.ANY)
    dma = pltpu.SemaphoreType.DMA
    params = pltpu.CompilerParams(vmem_limit_bytes=VMEM_LIMIT)
    products, inverse = pl.pallas_call(
        functools.partial(main_kernel, grid_rows, grid_cols),
        out_shape=(
            jax.ShapeDtypeStruct((2, 16, 8, 128), F32),
            jax.ShapeDtypeStruct((16, 128), I32),
        ),
        in_specs=[whole] * 3 + [left] * LOCAL_ARRAYS,
        out_specs=(whole,) * 2,
        scratch_shapes=[
            pltpu.VMEM((4, 4, 64, 128), BF16),
            pltpu.VMEM((4, 4, 9, 128, 128), BF16),
            pltpu.VMEM((4, 4, 64, 64), BF16),
            pltpu.VMEM((2, 2, 64, 64), BF16),
            pltpu.VMEM((1, 1, 64, 64), BF16),
            pltpu.VMEM((1, 4, 64, 64), BF16),
            pltpu.VMEM((4, 4, 36, 64, 64), BF16),
            pltpu.VMEM((2, 2, 36, 64, 64), BF16),
            pltpu.VMEM((1, 1, 36, 64, 64), BF16),
            pltpu.VMEM((1, 1, 36, 16, 64), BF16),
            pltpu.VMEM((16, 18, 64, 128), BF16),
            pltpu.VMEM((4, 18, 64, 128), BF16),
            pltpu.VMEM((64, 2304), BF16),
            pltpu.VMEM((4, 16, 2304), BF16),
            pltpu.VMEM((16, 16, 256), BF16),
            pltpu.VMEM((16, 256), F32),
            pltpu.VMEM((16, 256), BF16),
            pltpu.VMEM((256, 128), BF16),
            pltpu.VMEM((4, 64, 256), BF16),
            pltpu.VMEM((128, 1024), BF16),
            pltpu.VMEM((128, 2048), BF16),
            pltpu.VMEM((128, 128), BF16),
            pltpu.VMEM((128, 2048), BF16),
            pltpu.VMEM((8, 2304), F32),
            pltpu.VMEM((8, 2304), F32),
            pltpu.VMEM((8, 1024), F32),
            pltpu.VMEM((2, 8, 8, 16, 128), BF16),
            pltpu.VMEM((2, 2, 8, 8, 128), F32),
            pltpu.VMEM((2, 3, 6, 16, 128), BF16),
            pltpu.VMEM((2, 4, 2, 2, 8, 128), F32),
            pltpu.VMEM((2, 4, 4, 8, 128), F32),
            pltpu.VMEM((8, 4, 8, 128), F32),
            pltpu.VMEM((16, 8, 128), F32),
            pltpu.VMEM((4, 8, 256), F32),
            dma((LOCAL_ARRAYS,)),
            dma((2, 15)),
            dma((2, 15)),
            dma((2, 15)),
            dma((2, 15)),
            dma((2, 7)),
            dma((2, 7)),
            dma((2, 5)),
            dma((2, 5)),
            dma((2, 8)),
            dma((2, 8)),
            dma((3,)),
            dma((3,)),
            dma((2,)),
            dma((2,)),
            dma((14,)),
            dma((14,)),
        ],
        compiler_params=pltpu.CompilerParams(
            collective_id=0, has_side_effects=True, vmem_limit_bytes=VMEM_LIMIT
        ),
    )(
        jnp.transpose(values, (1, 2, 0, 3)),
        point_slot,
        coupling_top,
        jnp.swapaxes(leaf_basis, 2, 3),
        near_blocks,
        transfer_leaf,
        transfer_mid,
        transfer_dev,
        transfer_coarse,
        coupling_leaf,
        coupling_mid,
        coupling_dev,
        coupling_coarse,
    )
    placed = jax.ShapeDtypeStruct(values.shape, F32)
    return pl.pallas_call(
        place_kernel,
        out_shape=(placed, placed),
        in_specs=[left] * 2,
        out_specs=(left,) * 2,
        scratch_shapes=[
            pltpu.VMEM((2, 16, 8, 128), F32),
            pltpu.VMEM((16, 128), I32),
            pltpu.VMEM((2, 8, 1, 1, 2048), F32),
            dma((3,)),
            dma((2,)),
        ],
        compiler_params=params,
    )(products, inverse)


def solution(mesh):
    placed = (
        P(None, "gx", "gy", None),
        P("gx", "gy", None),
        P("gx", "gy", None, None),
        P("gx", "gy", None, None, None),
        P("gx", "gy", None, None),
        P("gx", "gy", None, None),
        P("gx", "gy", None, None),
        P(),
        P("gx", "gy", None, None, None),
        P("gx", "gy", None, None, None),
        P("gx", "gy", None, None, None),
        P("gx", "gy", None, None, None),
        P("gx", "gy", None, None, None),
    )
    return jax.shard_map(
        functools.partial(local, mesh.shape["gx"], mesh.shape["gy"]),
        mesh=mesh,
        in_specs=placed,
        out_specs=(P(None, "gx", "gy", None), P(None, "gx", "gy", None)),
        check_vma=False,
    )
```
